512 devices in a mesh: frame: 32 (over y, z_lo, core), patch: 16 (over x, z_hi).
Axes of the slice: x: 4, y: 4, z: 16 (z_hi: 4, z_lo: 4; z = z_hi * 4 + z_lo), core: 2. Of those that a mesh axis runs over, the one named last changes fastest.
Arguments:
- tokens: bfloat16 [32, 2048, 1152], P('frame', 'patch'), may hold values from -700 to 700, as said below
- key_frame: int32 [1], replicated, may hold values from 0 to 31
- qkv_spatial: bfloat16 [1152, 3456], P(None, 'patch'), may hold values from -10 to 10
- out_spatial: bfloat16 [1152, 1152], replicated, may hold values from -0.75 to 0.75
- qkv_temporal: bfloat16 [1152, 3456], P(None, 'patch'), may hold values from -10 to 10
Outputs:
- spatial_out: bfloat16 [32, 2048, 1152], P('frame', 'patch')
- temporal_out: bfloat16 [32, 2048, 1152], P('frame', 'patch')
The draws below stay inside these ranges and needn't reach their ends.
Inputs may be any that keep to these rules, and one draw needn't show every extreme that they name: `tokens`: patch features.
All inputs are finite; a program needn't handle non-finite values.
Results may differ from the reference program's by a relative error of at most 0.024.
Values may be sent and summed in bfloat16 or wider, within the bound.
A program may use at most 64 MiB of HBM per device.

```python
import math
import jax
import jax.numpy as jnp
from jax import lax

D = 1152
HEADS = 16
HEAD_DIM = 72
PATCHES = 2048
FRAMES = 32


def draw_tokens(key, part):
    key = jax.random.fold_in(key, 11)
    key_list = jax.random.split(key, 3)
    col_scale = jnp.exp(jax.random.uniform(key_list[0], (D,), jnp.float32) * math.log(10.0))
    row_scale = jnp.exp(jax.random.uniform(key_list[1], (FRAMES, PATCHES, 1), jnp.float32) * math.log(10.0))
    values = jax.random.truncated_normal(key_list[2], -6.0, 6.0, (FRAMES, PATCHES, D), jnp.float32)
    return (values * row_scale * col_scale).astype(jnp.bfloat16)


def qkv_weights(key):
    key_list = jax.random.split(key, 1)
    column_scale = jnp.array([2.0 ** 0.5, 2.0 ** 0.5, 1.0], jnp.float32)[None, None, :, None] / math.sqrt(D)
    entries = jax.random.truncated_normal(key_list[0], -6.0, 6.0, (D, HEADS, 3, HEAD_DIM), jnp.float32)
    return (entries * column_scale).reshape(D, 3 * D)


def draw_qkv_spatial(key, part):
    key = jax.random.fold_in(key, 21)
    return qkv_weights(key).astype(jnp.bfloat16)


def draw_qkv_temporal(key, part):
    key = jax.random.fold_in(key, 22)
    return qkv_weights(key).astype(jnp.bfloat16)


def scatter_about(stream_key, extent, width, limit, dtype=jnp.bfloat16):
    return jnp.clip(width * jax.random.normal(stream_key, extent, jnp.float32), -limit, limit).astype(dtype)


def setup_inputs(seed: int = 0) -> dict:
    streams_of = jax.random.split(jax.random.key(seed), 6)
    return {
        "tokens": draw_tokens(jax.random.fold_in(streams_of[5], 71), 0),
        "key_frame": jax.random.randint(streams_of[1], (1,), 0, FRAMES).astype(jnp.int32),
        "qkv_spatial": draw_qkv_spatial(jax.random.fold_in(streams_of[5], 71), 0),
        "out_spatial": scatter_about(streams_of[3], (D, D), HEAD_DIM ** -0.5, 0.75),
        "qkv_temporal": draw_qkv_temporal(jax.random.fold_in(streams_of[5], 71), 0),
    }


epsilon = 1e-06
highest = lax.Precision.HIGHEST

def rms_norm(values):
    values = values.astype(jnp.float32)
    return values * lax.rsqrt(lax.optimization_barrier(jnp.mean(values * values, axis=-1, keepdims=True)) + epsilon)

def softmax_rows(scores):
    largest = lax.optimization_barrier(jnp.max(scores, axis=-1, keepdims=True))
    exponent = jnp.exp(scores - largest)
    return (exponent / lax.optimization_barrier(jnp.sum(exponent, axis=-1, keepdims=True))).astype(jnp.bfloat16)

def project(frame_rows, matrix):
    normed = rms_norm(frame_rows).astype(jnp.bfloat16)
    return jnp.dot(normed, matrix, preferred_element_type=jnp.float32).astype(jnp.bfloat16)

def reference(tokens, key_frame, qkv_spatial, out_spatial, qkv_temporal):
    score_scale = HEAD_DIM ** (-0.5)
    key_rows = lax.dynamic_index_in_dim(tokens, key_frame[0].astype(jnp.int32), 0, keepdims=False)
    key_qkv = project(key_rows, qkv_spatial).reshape(PATCHES, HEADS, 3, HEAD_DIM).transpose(1, 2, 0, 3)

    def spatial_head(paired):
        own_qkv, frame_qkv = paired
        all_keys = jnp.concatenate([own_qkv[1], frame_qkv[1]], axis=0).astype(jnp.float32)
        all_values = jnp.concatenate([own_qkv[2], frame_qkv[2]], axis=0).astype(jnp.float32)
        scores = jnp.dot(own_qkv[0].astype(jnp.float32), all_keys.T, precision=highest) * score_scale
        weights = softmax_rows(scores)
        return jnp.dot(weights.astype(jnp.float32), all_values, precision=highest).astype(jnp.bfloat16)

    def spatial_frame(frame_rows):
        frame_qkv = project(frame_rows, qkv_spatial).reshape(PATCHES, HEADS, 3, HEAD_DIM).transpose(1, 2, 0, 3)
        heads_out = lax.map(spatial_head, (frame_qkv, key_qkv))
        merged = heads_out.transpose(1, 0, 2).reshape(PATCHES, D)
        return jnp.dot(merged, out_spatial, preferred_element_type=jnp.float32).astype(jnp.bfloat16)
    spatial_out = lax.map(spatial_frame, tokens)

    def temporal_project(frame_rows):
        return project(frame_rows, qkv_temporal)
    temporal_qkv = lax.map(temporal_project, spatial_out)
    temporal_qkv = temporal_qkv.reshape(FRAMES, PATCHES, HEADS, 3, HEAD_DIM).transpose(2, 3, 0, 1, 4)

    def temporal_head(split_qkv):
        query = split_qkv[0].astype(jnp.float32)
        own_keys = split_qkv[1].astype(jnp.float32)
        own_values = split_qkv[2].astype(jnp.float32)
        scores = jnp.einsum('fpc,gpc->pfg', query, own_keys, precision=highest) * score_scale
        weights = softmax_rows(scores)
        return jnp.einsum('pfg,gpc->fpc', weights.astype(jnp.float32), own_values, precision=highest).astype(jnp.bfloat16)
    temporal_heads = lax.map(temporal_head, temporal_qkv)
    temporal_out = temporal_heads.transpose(1, 2, 0, 3).reshape(FRAMES, PATCHES, D)
    return (spatial_out, temporal_out)
```

```python
import functools

import jax
import jax.numpy as jnp
from jax import lax
from jax.experimental import pallas as pl
from jax.experimental.pallas import tpu as pltpu
from jax.sharding import PartitionSpec as P

D = 1152
HEADS = 16
HEAD_DIM = 72
PATCHES = 2048
BLOCK = 128
LANES = 128
CHUNKS = 2
ROWS = BLOCK // CHUNKS
KEY_ROWS = 16
FRAGMENT = D // 8
epsilon = 1e-06
LOG2E = 1.4426950408889634
BF16 = jnp.bfloat16
F32 = jnp.float32


def rms_norm(values):
    values = values.astype(F32)
    return values * lax.rsqrt(jnp.mean(values * values, axis=-1, keepdims=True) + epsilon)


def places():
    patch, frame = lax.axis_index("patch"), lax.axis_index("frame")
    return (
        patch,
        frame,
        lax.div(patch, 4),
        lax.rem(patch, 4),
        lax.div(frame, 8),
        lax.rem(lax.div(frame, 2), 4),
        lax.rem(frame, 2),
    )


def turn(at, by):
    return lax.rem(at + by, 4)


class Links:
    def __init__(self, send, recv):
        self.send, self.recv, self.used, self.open = send, recv, 0, []
        self.patch, self.frame, self.x, self.zh, self.y, self.zl, self.core = places()

    def patch_device(self, dx, dz):
        return (self.frame, turn(self.x, dx) * 4 + turn(self.zh, dz))

    def frame_device(self, dy, dz, dc):
        frame = turn(self.y, dy) * 8 + turn(self.zl, dz) * 2 + lax.rem(self.core + dc, 2)
        return (frame, self.patch)

    def copy(self, src, dst, device):
        made = pltpu.make_async_remote_copy(
            src_ref=src,
            dst_ref=dst,
            send_sem=self.send.at[self.used],
            recv_sem=self.recv.at[self.used],
            device_id=device,
            device_id_type=pl.DeviceIdType.MESH,
        )
        made.start()
        self.used += 1
        self.open.append(made)
        return made

    def finish(self):
        for made in self.open:
            made.wait_send()


def greet(devices):
    barrier = pltpu.get_barrier_semaphore()
    for device in devices:
        pl.semaphore_signal(barrier, inc=1, device_id=device, device_id_type=pl.DeviceIdType.MESH)
    pl.semaphore_wait(barrier, len(devices))


class Gather:
    def __init__(self, links, held, rows):
        self.links, self.held, self.rows = links, held, rows
        self.along_x = {}
        self.last = {}

    def halves(self):
        if self.rows % 32:
            return [(pl.ds(0, self.rows), 0)]
        half = self.rows // 2
        return [(pl.ds(0, half), 0), (pl.ds(half, half), 1)]

    def send_x(self, dz):
        links, held = self.links, self.held
        self.along_x[dz] = (
            links.copy(held.at[dz, 0], held.at[dz, 3], links.patch_device(1, 0)),
            links.copy(held.at[dz, 0], held.at[dz, 1], links.patch_device(3, 0)),
        )

    def begin(self):
        links, held = self.links, self.held
        self.up = links.copy(held.at[0, 0], held.at[3, 0], links.patch_device(0, 1))
        self.down = links.copy(held.at[0, 0], held.at[1, 0], links.patch_device(0, 3))
        self.send_x(0)

    def neighbours(self):
        links, held = self.links, self.held
        self.far = []
        self.up.wait_recv()
        for part, way in self.halves():
            if way == 0:
                self.far.append(
                    links.copy(held.at[3, 0, part], held.at[2, 0, part], links.patch_device(0, 1))
                )
        self.send_x(3)
        self.down.wait_recv()
        for part, way in self.halves():
            if way == 1:
                self.far.append(
                    links.copy(held.at[1, 0, part], held.at[2, 0, part], links.patch_device(0, 3))
                )
        self.send_x(1)

    def opposite(self):
        for made in self.far:
            made.wait_recv()
        self.send_x(2)

    def forward_x(self, dz):
        links, held = self.links, self.held
        up, down = self.along_x[dz]
        self.last[dz] = []
        up.wait_recv()
        for part, way in self.halves():
            if way == 0:
                self.last[dz].append(
                    links.copy(held.at[dz, 3, part], held.at[dz, 2, part], links.patch_device(1, 0))
                )
        down.wait_recv()
        for part, way in self.halves():
            if way == 1:
                self.last[dz].append(
                    links.copy(held.at[dz, 1, part], held.at[dz, 2, part], links.patch_device(3, 0))
                )

    def done_x(self, dz):
        for made in self.last[dz]:
            made.wait_recv()


def with_ones(values):
    lane = lax.broadcasted_iota(jnp.int32, values.shape, 1)
    return jnp.where(lane == HEAD_DIM, jnp.ones_like(values), values)


GATHER_COPIES = 20
FIRST_COPIES = (CHUNKS + 1) * GATHER_COPIES + 7 + 3 + 7 + 12


def project_kernel(
    pick_ref,
    tokens_ref,
    w_ref,
    wt_ref,
    q_ref,
    k_ref,
    v_ref,
    wt4_ref,
    held0,
    held1,
    kheld,
    slices,
    first,
    second,
    kv_out,
    kv_in,
    wt4,
    send,
    recv,
    local_sem,
):
    links = Links(send, recv)
    others = [(dy, dc) for dy in range(4) for dc in range(2) if (dy, dc) != (0, 0)]
    greet(
        [links.patch_device(dx, dz) for dx, dz in ((1, 0), (3, 0), (0, 1), (0, 2), (0, 3))]
        + [links.frame_device(dy, 0, dc) for dy, dc in others]
        + [links.frame_device(0, dz, 0) for dz in (1, 2, 3)]
    )
    held = (held0, held1)
    normed = rms_norm(tokens_ref[...]).astype(BF16)
    for c in range(CHUNKS):
        held[c][0, 0] = normed[c * ROWS : (c + 1) * ROWS]
    for g in range(8):
        slices[g] = normed[g * KEY_ROWS : (g + 1) * KEY_ROWS]
    picks = []
    for dy, dc in others:
        there = turn(links.y, dy) * 2 + lax.rem(links.core + dc, 2)
        slot = (4 - dy) % 4 * 2 + dc
        picks.append(
            links.copy(slices.at[there], first.at[slot], links.frame_device(dy, 0, dc))
        )
    gathers = [Gather(links, held[c], ROWS) for c in range(CHUNKS)]
    gathers[0].begin()
    gathers[1].begin()
    part = pl.ds(pl.multiple_of((links.core * 4 + links.y) * FRAGMENT, 16), FRAGMENT)
    own = pltpu.make_async_copy(wt_ref.at[part], wt4.at[links.zh, part], local_sem)
    own.start()
    own.wait()
    wt_z = [
        links.copy(wt4.at[links.zh, part], wt4.at[links.zh, part], links.patch_device(0, dz))
        for dz in (1, 2, 3)
    ]
    here = links.y * 2 + links.core
    first[0] = slices[here]
    for made in picks:
        made.wait_recv()
    second[0] = first[pick_ref[0]]
    picks = [
        links.copy(second.at[0], second.at[4 - dz], links.frame_device(0, dz, 0))
        for dz in (1, 2, 3)
    ]
    for made in picks:
        made.wait_recv()
    kheld[0, 0] = second[pick_ref[1]]
    keys = Gather(links, kheld, KEY_ROWS)
    keys.begin()
    gathers[0].neighbours()
    keys.neighbours()
    gathers[1].neighbours()
    for made in wt_z:
        made.wait_recv()
    wt_y = [
        links.copy(wt4.at[:, part], wt4.at[:, part], links.frame_device(dy, 0, 0))
        for dy in (1, 3, 2)
    ]
    gathers[0].forward_x(0)
    gathers[1].forward_x(0)
    keys.forward_x(0)
    gathers[0].opposite()
    keys.opposite()
    gathers[1].opposite()

    def store(block, c, dz):
        out = jnp.dot(block, w_ref[...], preferred_element_type=F32)
        for dx in range(4):
            patch = turn(links.x, dx) * 4 + turn(links.zh, dz)
            at = pl.ds(pl.multiple_of(patch * BLOCK + c * ROWS, ROWS), ROWS)
            rows = out[dx * ROWS : (dx + 1) * ROWS]
            q_ref[at, :] = (rows[:, :LANES] * (HEAD_DIM**-0.5 * LOG2E)).astype(BF16)
            k_ref[at, :] = rows[:, LANES : 2 * LANES].astype(BF16)
            v_ref[at, :] = with_ones(rows[:, 2 * LANES :]).astype(BF16)

    def finish(dz):
        for c in range(CHUNKS):
            gathers[c].done_x(dz)
            store(held[c][dz].reshape(4 * ROWS, D), c, dz)

    for dz in (3, 1):
        for one in (gathers[0], keys, gathers[1]):
            one.forward_x(dz)
    keys.forward_x(2)
    finish(0)
    finish(3)
    for made in wt_y:
        made.wait_recv()
    half = pl.ds(pl.multiple_of(links.core * 4 * FRAGMENT, 16), 4 * FRAGMENT)
    wt_c = links.copy(wt4.at[:, half], wt4.at[:, half], links.frame_device(0, 0, 1))
    for dz in range(4):
        keys.done_x(dz)
    kv_out[...] = jnp.dot(
        kheld[...].reshape(16 * KEY_ROWS, D), w_ref[:, LANES:], preferred_element_type=F32
    ).astype(BF16)
    kv = [
        links.copy(kv_out, kv_in.at[(4 - dy) % 4 * 2 + dc], links.frame_device(dy, 0, dc))
        for dy, dc in others
    ]
    finish(1)
    for one in gathers:
        one.forward_x(2)
    finish(2)
    kv_in[0] = kv_out[...]
    for made in kv:
        made.wait_recv()
    for g in range(8):
        at = pl.ds(PATCHES + g * 16 * KEY_ROWS, 16 * KEY_ROWS)
        k_ref[at, :] = kv_in[g, :, :LANES]
        v_ref[at, :] = with_ones(kv_in[g, :, LANES:].astype(F32)).astype(BF16)
    wt_c.wait_recv()
    wt4_ref[...] = wt4[...]
    links.finish()


def project(pick, tokens, w, wt):
    vmem = pl.BlockSpec(memory_space=pltpu.VMEM)
    columns = wt.shape[1]
    return pl.pallas_call(
        project_kernel,
        out_shape=[
            jax.ShapeDtypeStruct((PATCHES, LANES), BF16),
            jax.ShapeDtypeStruct((2 * PATCHES, LANES), BF16),
            jax.ShapeDtypeStruct((2 * PATCHES, LANES), BF16),
            jax.ShapeDtypeStruct((4, D, columns), BF16),
        ],
        in_specs=[pl.BlockSpec(memory_space=pltpu.SMEM), vmem, vmem, vmem],
        out_specs=[vmem] * 4,
        scratch_shapes=[
            pltpu.VMEM((4, 4, ROWS, D), BF16),
            pltpu.VMEM((4, 4, ROWS, D), BF16),
            pltpu.VMEM((4, 4, KEY_ROWS, D), BF16),
            pltpu.VMEM((8, KEY_ROWS, D), BF16),
            pltpu.VMEM((8, KEY_ROWS, D), BF16),
            pltpu.VMEM((4, KEY_ROWS, D), BF16),
            pltpu.VMEM((16 * KEY_ROWS, 2 * LANES), BF16),
            pltpu.VMEM((8, 16 * KEY_ROWS, 2 * LANES), BF16),
            pltpu.VMEM((4, D, columns), BF16),
            pltpu.SemaphoreType.DMA((FIRST_COPIES,)),
            pltpu.SemaphoreType.DMA((FIRST_COPIES,)),
            pltpu.SemaphoreType.DMA,
        ],
        compiler_params=pltpu.CompilerParams(
            collective_id=1, has_side_effects=True, vmem_limit_bytes=48 * 2**20
        ),
        name="project",
    )(pick, tokens, w, wt)


Q_ROWS = 256
KEY_STEP = 2048


def attend_kernel(q_ref, k_ref, v_ref, wt4_ref, o_ref, wt_ref, kt, send, recv, local_sem):
    links = Links(send, recv)
    greet([links.patch_device(1, 0), links.patch_device(3, 0), links.frame_device(0, 0, 1)])
    x = links.x
    mine = pl.ds(pl.multiple_of(links.core * (D // 2), 16), D // 2)

    def group(at):
        return pl.ds(at * 4, 4)

    up = links.copy(wt4_ref.at[:, mine], wt_ref.at[group(x), mine], links.patch_device(1, 0))
    down = links.copy(wt4_ref.at[:, mine], wt_ref.at[group(x), mine], links.patch_device(3, 0))
    own = pltpu.make_async_copy(wt4_ref, wt_ref.at[group(x)], local_sem)
    own.start()
    for j in range(2 * PATCHES // 512):
        kt[:, j * 512 : (j + 1) * 512] = k_ref[j * 512 : (j + 1) * 512, :].T

    def rows_of(i):
        q = q_ref[pl.ds(pl.multiple_of(i * Q_ROWS, Q_ROWS), Q_ROWS), :]
        total = largest = None
        for j in range(2 * PATCHES // KEY_STEP):
            keys = slice(j * KEY_STEP, (j + 1) * KEY_STEP)
            scores = jnp.dot(q, kt[:, keys], preferred_element_type=F32)
            new = jnp.max(scores, axis=-1, keepdims=True)
            if j:
                new = jnp.maximum(largest, new)
            weights = jnp.exp2(scores - new).astype(BF16)
            part = jnp.dot(weights, v_ref[keys, :], preferred_element_type=F32)
            total = part if j == 0 else total * jnp.exp2(largest - new) + part
            largest = new
        out = total / total[:, HEAD_DIM : HEAD_DIM + 1]
        turned = out.T
        for b in range(Q_ROWS // BLOCK):
            o_ref[i * (Q_ROWS // BLOCK) + b] = turned[:HEAD_DIM, b * BLOCK : (b + 1) * BLOCK].astype(BF16)

    def loop(first, last):
        pl.loop(first, last)(rows_of)

    steps = PATCHES // Q_ROWS
    loop(0, steps // 2)
    own.wait()
    quarter = D // 4
    up.wait_recv()
    lower = pl.ds(pl.multiple_of(links.core * (D // 2), 16), quarter)
    upper = pl.ds(pl.multiple_of(links.core * (D // 2) + quarter, 16), quarter)
    left, right = group(turn(x, 3)), group(turn(x, 1))
    far = [links.copy(wt_ref.at[left, lower], wt_ref.at[left, lower], links.patch_device(1, 0))]
    other = links.frame_device(0, 0, 1)
    cross = [links.copy(wt_ref.at[left, mine], wt_ref.at[left, mine], other)]
    down.wait_recv()
    far.append(links.copy(wt_ref.at[right, upper], wt_ref.at[right, upper], links.patch_device(3, 0)))
    cross.append(links.copy(wt_ref.at[right, mine], wt_ref.at[right, mine], other))
    loop(steps // 2, steps)
    for made in far:
        made.wait_recv()
    opposite = group(turn(x, 2))
    cross.append(links.copy(wt_ref.at[opposite, mine], wt_ref.at[opposite, mine], other))
    for made in cross:
        made.wait_recv()
    links.finish()


def attend(q, k, v, wt4):
    vmem = pl.BlockSpec(memory_space=pltpu.VMEM)
    anywhere = pl.BlockSpec(memory_space=pl.ANY)
    columns = wt4.shape[2]
    return pl.pallas_call(
        attend_kernel,
        out_shape=[
            jax.ShapeDtypeStruct((HEADS, HEAD_DIM, BLOCK), BF16),
            jax.ShapeDtypeStruct((HEADS, D, columns), BF16),
        ],
        in_specs=[vmem, vmem, vmem, anywhere],
        out_specs=[vmem, anywhere],
        scratch_shapes=[
            pltpu.VMEM((LANES, 2 * PATCHES), BF16),
            pltpu.SemaphoreType.DMA((7,)),
            pltpu.SemaphoreType.DMA((7,)),
            pltpu.SemaphoreType.DMA,
        ],
        compiler_params=pltpu.CompilerParams(
            collective_id=2, has_side_effects=True, vmem_limit_bytes=48 * 2**20
        ),
        name="attend",
    )(q, k, v, wt4)


def temporal_kernel(x_ref, wt_ref, o_ref, turned):
    x = x_ref[...]
    row = lax.broadcasted_iota(jnp.int32, (BLOCK, BLOCK), 0)
    column = lax.broadcasted_iota(jnp.int32, (BLOCK, BLOCK), 1)
    same = (row & 3) == (column & 3)
    for h in range(HEADS):
        qkv = jnp.dot(x, wt_ref[h], preferred_element_type=F32).astype(BF16)
        q, k, v = (qkv[:, i * HEAD_DIM : (i + 1) * HEAD_DIM] for i in range(3))
        scores = lax.dot_general(
            q, k, (((1,), (1,)), ((), ())), preferred_element_type=F32
        ) * (HEAD_DIM**-0.5)
        scores = jnp.where(same, scores, -jnp.inf)
        exponent = jnp.exp(scores - jnp.max(scores, axis=-1, keepdims=True))
        weights = (exponent / jnp.sum(exponent, axis=-1, keepdims=True)).astype(BF16)
        out = jnp.dot(weights, v, preferred_element_type=F32)
        turned[h * HEAD_DIM : (h + 1) * HEAD_DIM, :] = out.T
    o_ref[...] = turned[...].T.astype(BF16)


def temporal_attend(x, wt):
    vmem = pl.BlockSpec(memory_space=pltpu.VMEM)
    return pl.pallas_call(
        temporal_kernel,
        out_shape=jax.ShapeDtypeStruct((BLOCK, D), BF16),
        in_specs=[vmem, vmem],
        out_specs=vmem,
        scratch_shapes=[pltpu.VMEM((D, BLOCK), F32)],
        compiler_params=pltpu.CompilerParams(vmem_limit_bytes=48 * 2**20),
        name="temporal_attend",
    )(x, wt)


def per_device(tokens, key_frame, qkv_spatial, out_spatial, qkv_temporal):
    frame = lax.axis_index("frame")
    key = key_frame[0].astype(jnp.int32)
    y, zl, core = frame // 8, (frame // 2) % 4, frame % 2
    pick = jnp.stack(
        [(key // 8 - y) % 4 * 2 + (key % 2 - core) % 2, (key // 2 % 4 - zl) % 4]
    ).astype(jnp.int32)
    w = qkv_spatial.reshape(D, 3, HEAD_DIM)
    w = jnp.pad(w, ((0, 0), (0, 0), (0, LANES - HEAD_DIM))).reshape(D, 3 * LANES)
    q, k, v, wt4 = project(pick, tokens[0], w, qkv_temporal)
    heads, wt = attend(q, k, v, wt4)
    heads = lax.all_to_all(heads, "patch", split_axis=0, concat_axis=0, tiled=True)
    spatial = lax.dot_general(
        heads.reshape(D, BLOCK), out_spatial, (((0,), (0,)), ((), ())), preferred_element_type=F32
    ).astype(BF16)
    temporal_in = rms_norm(spatial).astype(BF16)
    rows = lax.all_to_all(
        temporal_in.reshape(32, 4, D), "frame", split_axis=0, concat_axis=0, tiled=True
    )
    mixed = temporal_attend(rows.reshape(BLOCK, D), wt)
    temporal = lax.all_to_all(
        mixed.reshape(32, 4, D), "frame", split_axis=0, concat_axis=0, tiled=True
    )
    return (spatial[None], temporal.reshape(1, BLOCK, D))


def solution(mesh):
    return jax.shard_map(
        per_device,
        mesh=mesh,
        in_specs=(P("frame", "patch", None), P(), P(None, "patch"), P(), P(None, "patch")),
        out_specs=(P("frame", "patch", None), P("frame", "patch", None)),
        check_vma=False,
    )
```

```python
import functools

import jax
import jax.numpy as jnp
from jax import lax
from jax.experimental import pallas as pl
from jax.experimental.pallas import tpu as pltpu
from jax.sharding import PartitionSpec as P

D = 1152
HEADS = 16
HEAD_DIM = 72
PATCHES = 2048
BLOCK = 128
LANES = 128
CHUNKS = 2
ROWS = BLOCK // CHUNKS
KEY_ROWS = 16
FRAGMENT = D // 8
epsilon = 1e-06
LOG2E = 1.4426950408889634
BF16 = jnp.bfloat16
F32 = jnp.float32


def rms_norm(values):
    values = values.astype(F32)
    return values * lax.rsqrt(jnp.mean(values * values, axis=-1, keepdims=True) + epsilon)


def places():
    patch, frame = lax.axis_index("patch"), lax.axis_index("frame")
    return (
        patch,
        frame,
        lax.div(patch, 4),
        lax.rem(patch, 4),
        lax.div(frame, 8),
        lax.rem(lax.div(frame, 2), 4),
        lax.rem(frame, 2),
    )


def turn(at, by):
    return lax.rem(at + by, 4)


class Links:
    def __init__(self, send, recv):
        self.send, self.recv, self.used, self.open = send, recv, 0, []
        self.patch, self.frame, self.x, self.zh, self.y, self.zl, self.core = places()

    def patch_device(self, dx, dz):
        return (self.frame, turn(self.x, dx) * 4 + turn(self.zh, dz))

    def frame_device(self, dy, dz, dc):
        frame = turn(self.y, dy) * 8 + turn(self.zl, dz) * 2 + lax.rem(self.core + dc, 2)
        return (frame, self.patch)

    def copy(self, src, dst, device):
        made = pltpu.make_async_remote_copy(
            src_ref=src,
            dst_ref=dst,
            send_sem=self.send.at[self.used],
            recv_sem=self.recv.at[self.used],
            device_id=device,
            device_id_type=pl.DeviceIdType.MESH,
        )
        made.start()
        self.used += 1
        self.open.append(made)
        return made

    def finish(self):
        for made in self.open:
            made.wait_send()


def greet(devices):
    barrier = pltpu.get_barrier_semaphore()
    for device in devices:
        pl.semaphore_signal(barrier, inc=1, device_id=device, device_id_type=pl.DeviceIdType.MESH)
    pl.semaphore_wait(barrier, len(devices))


class Gather:
    def __init__(self, links, held, rows):
        self.links, self.held, self.rows = links, held, rows
        self.along_x = {}
        self.last = {}

    def halves(self):
        if self.rows % 32:
            return [(pl.ds(0, self.rows), 0)]
        half = self.rows // 2
        return [(pl.ds(0, half), 0), (pl.ds(half, half), 1)]

    def send_x(self, dz):
        links, held = self.links, self.held
        self.along_x[dz] = (
            links.copy(held.at[dz, 0], held.at[dz, 3], links.patch_device(1, 0)),
            links.copy(held.at[dz, 0], held.at[dz, 1], links.patch_device(3, 0)),
        )

    def begin_z(self):
        links, held = self.links, self.held
        self.up = links.copy(held.at[0, 0], held.at[3, 0], links.patch_device(0, 1))
        self.down = links.copy(held.at[0, 0], held.at[1, 0], links.patch_device(0, 3))

    def neighbours(self):
        links, held = self.links, self.held
        self.far = []
        self.up.wait_recv()
        for part, way in self.halves():
            if way == 0:
                self.far.append(
                    links.copy(held.at[3, 0, part], held.at[2, 0, part], links.patch_device(0, 1))
                )
        self.send_x(3)
        self.down.wait_recv()
        for part, way in self.halves():
            if way == 1:
                self.far.append(
                    links.copy(held.at[1, 0, part], held.at[2, 0, part], links.patch_device(0, 3))
                )
        self.send_x(1)

    def opposite(self):
        for made in self.far:
            made.wait_recv()
        self.send_x(2)

    def forward_x(self, dz):
        links, held = self.links, self.held
        up, down = self.along_x[dz]
        self.last[dz] = []
        up.wait_recv()
        for part, way in self.halves():
            if way == 0:
                self.last[dz].append(
                    links.copy(held.at[dz, 3, part], held.at[dz, 2, part], links.patch_device(1, 0))
                )
        down.wait_recv()
        for part, way in self.halves():
            if way == 1:
                self.last[dz].append(
                    links.copy(held.at[dz, 1, part], held.at[dz, 2, part], links.patch_device(3, 0))
                )

    def done_x(self, dz):
        for made in self.last[dz]:
            made.wait_recv()


def with_ones(values):
    lane = lax.broadcasted_iota(jnp.int32, values.shape, 1)
    return jnp.where(lane == HEAD_DIM, jnp.ones_like(values), values)


GATHER_COPIES = 20
COPIES = (CHUNKS + 1) * GATHER_COPIES + 7 + 3 + 7 + 3 + 6 + 6 + 8 + 15
SPLIT = 80
GROUP = 512


def spatial_kernel(
    pick_ref,
    tokens_ref,
    w_ref,
    wt_ref,
    out_w_ref,
    spatial_ref,
    normed_ref,
    wt,
    held0,
    held1,
    kheld,
    slices,
    first,
    second,
    w,
    q_s,
    kt,
    v_s,
    kv_out,
    kv_in,
    total_s,
    largest_s,
    out_s,
    heads,
    send,
    recv,
    local_sem,
):
    links = Links(send, recv)
    x, y, core = links.x, links.y, links.core
    others = [(dy, dc) for dy in range(4) for dc in range(2) if (dy, dc) != (0, 0)]
    turns = [(dz, dx) for dz in (0, 3, 1, 2) for dx in range(4)]
    greet(
        [links.patch_device(dx, dz) for dz, dx in turns if (dz, dx) != (0, 0)]
        + [links.frame_device(dy, 0, dc) for dy, dc in others]
        + [links.frame_device(0, dz, 0) for dz in (1, 2, 3)]
    )
    held = (held0, held1)
    normed = rms_norm(tokens_ref[...]).astype(BF16)
    for g in range(8):
        slices[g] = normed[g * KEY_ROWS : (g + 1) * KEY_ROWS]
    picks = []
    for dy, dc in others:
        there = turn(y, dy) * 2 + lax.rem(core + dc, 2)
        slot = (4 - dy) % 4 * 2 + dc
        picks.append(
            links.copy(slices.at[there], first.at[slot], links.frame_device(dy, 0, dc))
        )
    for c in range(CHUNKS):
        held[c][0, 0] = normed[c * ROWS : (c + 1) * ROWS]
    gathers = [Gather(links, held[c], ROWS) for c in range(CHUNKS)]
    for one in gathers:
        one.send_x(0)
    mine = wt_ref.at[pl.ds(pl.multiple_of((core * 4 + y) * FRAGMENT, 16), FRAGMENT)]
    place = wt.at[links.patch, core, y]
    own = pltpu.make_async_copy(mine, place, local_sem)
    own.start()
    first[0] = slices[y * 2 + core]
    for made in picks:
        made.wait_recv()
    second[0] = first[pick_ref[0]]
    picks = [
        links.copy(second.at[0], second.at[4 - dz], links.frame_device(0, dz, 0))
        for dz in (1, 2, 3)
    ]
    for one in gathers:
        one.begin_z()
    wt_up = links.copy(mine, place, links.patch_device(0, 1))
    wt_down = links.copy(mine, place, links.patch_device(0, 3))
    w[...] = jnp.zeros_like(w)
    for i in range(3):
        w[:, i * LANES : i * LANES + HEAD_DIM] = w_ref[:, i * HEAD_DIM : (i + 1) * HEAD_DIM]
    for made in picks:
        made.wait_recv()
    kheld[0, 0] = second[pick_ref[1]]
    keys = Gather(links, kheld, KEY_ROWS)
    keys.send_x(0)
    keys.begin_z()
    for one in gathers:
        one.forward_x(0)
    for one in (gathers[0], gathers[1], keys):
        one.neighbours()
    wt_up.wait_recv()
    below = wt.at[x * 4 + turn(links.zh, 3), core, y]
    wt_far = links.copy(below, below, links.patch_device(0, 1))
    keys.forward_x(0)

    def finish(dz):
        for c in range(CHUNKS):
            gathers[c].done_x(dz)
            out = jnp.dot(
                held[c][dz].reshape(4 * ROWS, D), w[...], preferred_element_type=F32
            )
            q = (out[:, :LANES] * (HEAD_DIM**-0.5 * LOG2E)).astype(BF16)
            for dx in range(4):
                at = (dz * 4 + dx) * BLOCK + c * ROWS
                q_s[at : at + ROWS, :] = q[dx * ROWS : (dx + 1) * ROWS]
            at = (dz * CHUNKS + c) * 4 * ROWS
            kt[:, at : at + 4 * ROWS] = out[:, LANES : 2 * LANES].T.astype(BF16)
            v_s[at : at + 4 * ROWS, :] = with_ones(out[:, 2 * LANES :]).astype(BF16)

    finish(0)
    for dz in (3, 1):
        for one in (gathers[0], gathers[1], keys):
            one.forward_x(dz)
    for one in (gathers[0], gathers[1], keys):
        one.opposite()
    own.wait()
    wt_down.wait_recv()
    wt_far.wait_recv()
    group = pl.ds(x * 4, 4)
    upper, lower = pl.ds(0, SPLIT), pl.ds(SPLIT, FRAGMENT - SPLIT)
    by_y, by_x = wt.at[group, core, y, upper], wt.at[group, core, y, lower]
    steps = []
    for d in (1, 3, 2):
        steps.append(links.copy(by_y, by_y, links.frame_device(d, 0, 0)))
        steps.append(links.copy(by_x, by_x, links.patch_device(d, 0)))
    finish(3)
    finish(1)
    for one in (gathers[0], gathers[1], keys):
        one.forward_x(2)
    for dz in range(4):
        keys.done_x(dz)
    kv_out[...] = jnp.dot(
        kheld[...].reshape(16 * KEY_ROWS, D), w[:, LANES:], preferred_element_type=F32
    ).astype(BF16)
    kv = [
        links.copy(kv_out, kv_in.at[(4 - dy) % 4 * 2 + dc], links.frame_device(dy, 0, dc))
        for dy, dc in others
    ]
    finish(2)
    for made in steps:
        made.wait_recv()
    def along_x(dx, rows=upper, half=slice(0, 4)):
        return wt.at[pl.ds(turn(x, dx) * 4, 4), core, pl.ds(half.start, half.stop - half.start), rows]

    def along_y(dy, half=slice(0, 16)):
        return wt.at[pl.ds(half.start, half.stop - half.start), core, turn(y, dy), lower]

    def pass_on(piece, device):
        return links.copy(piece, piece, device)

    twin = links.frame_device(0, 0, 1)
    x_up = pass_on(along_x(0), links.patch_device(1, 0))
    x_down = pass_on(along_x(0), links.patch_device(3, 0))
    y_up = pass_on(along_y(0), links.frame_device(1, 0, 0))
    y_down = pass_on(along_y(0), links.frame_device(3, 0, 0))
    cross = [pass_on(along_x(0), twin), pass_on(along_y(0), twin)]

    def scores_of(g, keys):
        q = q_s[g * GROUP : (g + 1) * GROUP, :]
        scores = jnp.dot(q, kt[:, keys], preferred_element_type=F32)
        return scores, jnp.max(scores, axis=-1, keepdims=True)

    for g in range(4):
        scores, largest = scores_of(g, slice(0, PATCHES))
        weights = jnp.exp2(scores - largest).astype(BF16)
        total_s[g] = jnp.dot(weights, v_s[:PATCHES, :], preferred_element_type=F32)
        largest_s[g] = jnp.broadcast_to(largest, (GROUP, LANES))
    kv_in[0] = kv_out[...]
    for made in kv:
        made.wait_recv()
    for g in range(8):
        at = PATCHES + g * 16 * KEY_ROWS
        kt[:, at : at + 16 * KEY_ROWS] = kv_in[g, :, :LANES].T
        v_s[at : at + 16 * KEY_ROWS, :] = with_ones(kv_in[g, :, LANES:].astype(F32)).astype(BF16)
    sent = []
    for i, g in enumerate((2, 3, 1, 0)):
        scores, new = scores_of(g, slice(PATCHES, 2 * PATCHES))
        largest = largest_s[g][:, :1]
        new = jnp.maximum(largest, new)
        weights = jnp.exp2(scores - new).astype(BF16)
        total = total_s[g] * jnp.exp2(largest - new) + jnp.dot(
            weights, v_s[PATCHES:, :], preferred_element_type=F32
        )
        turned = (total / total[:, HEAD_DIM : HEAD_DIM + 1]).T
        for dx in (2, 1, 3, 0):
            block = turned[:HEAD_DIM, dx * BLOCK : (dx + 1) * BLOCK].astype(BF16)
            if (g, dx) == (0, 0):
                heads[links.patch] = block
            else:
                out_s[g * 4 + dx] = block
                sent.append(
                    links.copy(
                        out_s.at[g * 4 + dx], heads.at[links.patch], links.patch_device(dx, g)
                    )
                )
        if i == 1:
            x_up.wait_recv()
            far = [pass_on(along_x(3, half=slice(0, 2)), links.patch_device(1, 0))]
            cross.append(pass_on(along_x(3), twin))
            y_up.wait_recv()
            far.append(pass_on(along_y(3, slice(0, 8)), links.frame_device(1, 0, 0)))
            cross.append(pass_on(along_y(3), twin))
            x_down.wait_recv()
            far.append(pass_on(along_x(1, half=slice(2, 4)), links.patch_device(3, 0)))
            cross.append(pass_on(along_x(1), twin))
            y_down.wait_recv()
            far.append(pass_on(along_y(1, slice(8, 16)), links.frame_device(3, 0, 0)))
            cross.append(pass_on(along_y(1), twin))
    for made in sent:
        made.wait_recv()
    rows = heads[...].reshape(D, BLOCK).T
    spatial = jnp.dot(rows, out_w_ref[...], preferred_element_type=F32).astype(BF16)
    spatial_ref[...] = spatial
    normed_ref[...] = rms_norm(spatial).astype(BF16)
    for made in far:
        made.wait_recv()
    cross.append(pass_on(along_x(2), twin))
    cross.append(pass_on(along_y(2), twin))
    for made in cross:
        made.wait_recv()
    links.finish()


def spatial_branch(pick, tokens, w, wt, out_w):
    vmem = pl.BlockSpec(memory_space=pltpu.VMEM)
    anywhere = pl.BlockSpec(memory_space=pl.ANY)
    columns = wt.shape[1]
    return pl.pallas_call(
        spatial_kernel,
        out_shape=[
            jax.ShapeDtypeStruct((BLOCK, D), BF16),
            jax.ShapeDtypeStruct((BLOCK, D), BF16),
            jax.ShapeDtypeStruct((HEADS, 2, 4, FRAGMENT, columns), BF16),
        ],
        in_specs=[pl.BlockSpec(memory_space=pltpu.SMEM), vmem, vmem, anywhere, vmem],
        out_specs=[vmem, vmem, anywhere],
        scratch_shapes=[
            pltpu.VMEM((4, 4, ROWS, D), BF16),
            pltpu.VMEM((4, 4, ROWS, D), BF16),
            pltpu.VMEM((4, 4, KEY_ROWS, D), BF16),
            pltpu.VMEM((8, KEY_ROWS, D), BF16),
            pltpu.VMEM((8, KEY_ROWS, D), BF16),
            pltpu.VMEM((4, KEY_ROWS, D), BF16),
            pltpu.VMEM((D, 3 * LANES), BF16),
            pltpu.VMEM((PATCHES, LANES), BF16),
            pltpu.VMEM((LANES, 2 * PATCHES), BF16),
            pltpu.VMEM((2 * PATCHES, LANES), BF16),
            pltpu.VMEM((16 * KEY_ROWS, 2 * LANES), BF16),
            pltpu.VMEM((8, 16 * KEY_ROWS, 2 * LANES), BF16),
            pltpu.VMEM((4, GROUP, LANES), F32),
            pltpu.VMEM((4, GROUP, LANES), F32),
            pltpu.VMEM((HEADS, HEAD_DIM, BLOCK), BF16),
            pltpu.VMEM((HEADS, HEAD_DIM, BLOCK), BF16),
            pltpu.SemaphoreType.DMA((COPIES,)),
            pltpu.SemaphoreType.DMA((COPIES,)),
            pltpu.SemaphoreType.DMA,
        ],
        compiler_params=pltpu.CompilerParams(
            collective_id=1, has_side_effects=True, vmem_limit_bytes=50 * 2**20
        ),
        name="spatial_branch",
    )(pick, tokens, w, wt, out_w)


HEAD_STEP = 4


def temporal_kernel(x_ref, wt_ref, o_ref, turned):
    step = pl.program_id(0)
    x = x_ref[...]
    row = lax.broadcasted_iota(jnp.int32, (BLOCK, BLOCK), 0)
    column = lax.broadcasted_iota(jnp.int32, (BLOCK, BLOCK), 1)
    same = (row & 3) == (column & 3)
    for h in range(HEAD_STEP):
        w = wt_ref[h].reshape(D, 3 * HEAD_DIM)
        qkv = jnp.dot(x, w, preferred_element_type=F32).astype(BF16)
        q, k = qkv[:, :HEAD_DIM], qkv[:, HEAD_DIM : 2 * HEAD_DIM]
        scores = lax.dot_general(
            q, k, (((1,), (1,)), ((), ())), preferred_element_type=F32
        ) * (HEAD_DIM**-0.5)
        scores = jnp.where(same, scores, -jnp.inf)
        exponent = jnp.exp(scores - jnp.max(scores, axis=-1, keepdims=True))
        weights = (exponent / jnp.sum(exponent, axis=-1, keepdims=True)).astype(BF16)
        out = jnp.dot(weights, qkv, preferred_element_type=F32)
        turned[step * HEAD_STEP + h] = out.T[2 * HEAD_DIM :, :]

    @pl.when(step == HEADS // HEAD_STEP - 1)
    def _():
        o_ref[...] = turned[...].reshape(D, BLOCK).T.astype(BF16)


def temporal_attend(x, wt):
    whole = pl.BlockSpec((BLOCK, D), lambda i: (0, 0))
    return pl.pallas_call(
        temporal_kernel,
        grid=(HEADS // HEAD_STEP,),
        out_shape=jax.ShapeDtypeStruct((BLOCK, D), BF16),
        in_specs=[
            whole,
            pl.BlockSpec((HEAD_STEP,) + wt.shape[1:], lambda i: (i, 0, 0, 0, 0)),
        ],
        out_specs=whole,
        scratch_shapes=[pltpu.VMEM((HEADS, HEAD_DIM, BLOCK), F32)],
        compiler_params=pltpu.CompilerParams(vmem_limit_bytes=48 * 2**20),
        name="temporal_attend",
    )(x, wt)


def per_device(tokens, key_frame, qkv_spatial, out_spatial, qkv_temporal):
    frame = lax.axis_index("frame")
    key = key_frame[0].astype(jnp.int32)
    y, zl, core = frame // 8, (frame // 2) % 4, frame % 2
    pick = jnp.stack(
        [(key // 8 - y) % 4 * 2 + (key % 2 - core) % 2, (key // 2 % 4 - zl) % 4]
    ).astype(jnp.int32)
    spatial, temporal_in, wt = spatial_branch(
        pick, tokens[0], qkv_spatial, qkv_temporal, out_spatial
    )
    rows = lax.all_to_all(
        temporal_in.reshape(32, 4, D), "frame", split_axis=0, concat_axis=0, tiled=True
    )
    mixed = temporal_attend(rows.reshape(BLOCK, D), wt)
    temporal = lax.all_to_all(
        mixed.reshape(32, 4, D), "frame", split_axis=0, concat_axis=0, tiled=True
    )
    return (spatial[None], temporal.reshape(1, BLOCK, D))


def solution(mesh):
    return jax.shard_map(
        per_device,
        mesh=mesh,
        in_specs=(P("frame", "patch", None), P(), P(None, "patch"), P(), P(None, "patch")),
        out_specs=(P("frame", "patch", None), P("frame", "patch", None)),
        check_vma=False,
    )
```

```python
import functools

import jax
import jax.numpy as jnp
from jax import lax
from jax.experimental import pallas as pl
from jax.experimental.pallas import tpu as pltpu
from jax.sharding import PartitionSpec as P

D = 1152
HEADS = 16
HEAD_DIM = 72
PATCHES = 2048
BLOCK = 128
LANES = 128
CHUNKS = 2
ROWS = BLOCK // CHUNKS
KEY_ROWS = 16
FRAGMENT = D // 8
epsilon = 1e-06
LOG2E = 1.4426950408889634
BF16 = jnp.bfloat16
F32 = jnp.float32


def rms_norm(values):
    values = values.astype(F32)
    return values * lax.rsqrt(jnp.mean(values * values, axis=-1, keepdims=True) + epsilon)


def places():
    patch, frame = lax.axis_index("patch"), lax.axis_index("frame")
    return (
        patch,
        frame,
        lax.div(patch, 4),
        lax.rem(patch, 4),
        lax.div(frame, 8),
        lax.rem(lax.div(frame, 2), 4),
        lax.rem(frame, 2),
    )


def turn(at, by):
    return lax.rem(at + by, 4)


class Links:
    def __init__(self, send, recv):
        self.send, self.recv, self.used, self.open = send, recv, 0, []
        self.patch, self.frame, self.x, self.zh, self.y, self.zl, self.core = places()

    def patch_device(self, dx, dz):
        return (self.frame, turn(self.x, dx) * 4 + turn(self.zh, dz))

    def frame_device(self, dy, dz, dc):
        frame = turn(self.y, dy) * 8 + turn(self.zl, dz) * 2 + lax.rem(self.core + dc, 2)
        return (frame, self.patch)

    def copy(self, src, dst, device):
        made = pltpu.make_async_remote_copy(
            src_ref=src,
            dst_ref=dst,
            send_sem=self.send.at[self.used],
            recv_sem=self.recv.at[self.used],
            device_id=device,
            device_id_type=pl.DeviceIdType.MESH,
        )
        made.start()
        self.used += 1
        self.open.append(made)
        return made

    def finish(self):
        for made in self.open:
            made.wait_send()


def greet(devices):
    barrier = pltpu.get_barrier_semaphore()
    for device in devices:
        pl.semaphore_signal(barrier, inc=1, device_id=device, device_id_type=pl.DeviceIdType.MESH)
    pl.semaphore_wait(barrier, len(devices))


class Gather:
    def __init__(self, links, held, rows):
        self.links, self.held, self.rows = links, held, rows
        self.along_x = {}
        self.last = {}

    def halves(self):
        if self.rows % 32:
            return [(pl.ds(0, self.rows), 0)]
        half = self.rows // 2
        return [(pl.ds(0, half), 0), (pl.ds(half, half), 1)]

    def send_x(self, dz):
        links, held = self.links, self.held
        self.along_x[dz] = (
            links.copy(held.at[dz, 0], held.at[dz, 3], links.patch_device(1, 0)),
            links.copy(held.at[dz, 0], held.at[dz, 1], links.patch_device(3, 0)),
        )

    def begin_z(self):
        links, held = self.links, self.held
        self.up = links.copy(held.at[0, 0], held.at[3, 0], links.patch_device(0, 1))
        self.down = links.copy(held.at[0, 0], held.at[1, 0], links.patch_device(0, 3))

    def neighbours(self):
        links, held = self.links, self.held
        self.far = []
        self.up.wait_recv()
        for part, way in self.halves():
            if way == 0:
                self.far.append(
                    links.copy(held.at[3, 0, part], held.at[2, 0, part], links.patch_device(0, 1))
                )
        self.send_x(3)
        self.down.wait_recv()
        for part, way in self.halves():
            if way == 1:
                self.far.append(
                    links.copy(held.at[1, 0, part], held.at[2, 0, part], links.patch_device(0, 3))
                )
        self.send_x(1)

    def opposite(self):
        for made in self.far:
            made.wait_recv()
        self.send_x(2)

    def forward_x(self, dz):
        links, held = self.links, self.held
        up, down = self.along_x[dz]
        self.last[dz] = []
        up.wait_recv()
        for part, way in self.halves():
            if way == 0:
                self.last[dz].append(
                    links.copy(held.at[dz, 3, part], held.at[dz, 2, part], links.patch_device(1, 0))
                )
        down.wait_recv()
        for part, way in self.halves():
            if way == 1:
                self.last[dz].append(
                    links.copy(held.at[dz, 1, part], held.at[dz, 2, part], links.patch_device(3, 0))
                )

    def done_x(self, dz):
        for made in self.last[dz]:
            made.wait_recv()


def with_ones(values):
    lane = lax.broadcasted_iota(jnp.int32, values.shape, 1)
    return jnp.where(lane == HEAD_DIM, jnp.ones_like(values), values)


GATHER_COPIES = 20
COPIES = (CHUNKS + 1) * GATHER_COPIES + 7 + 3 + 7 + 3 + 6 + 6 + 8 + 15
SPLIT = 80
GROUP = 512


def spatial_kernel(
    pick_ref,
    tokens_ref,
    w_ref,
    wt_ref,
    out_w_ref,
    spatial_ref,
    normed_ref,
    wt,
    held0,
    held1,
    kheld,
    slices,
    first,
    second,
    w,
    q_s,
    kt,
    v_s,
    kv_out,
    kv_in,
    total_s,
    largest_s,
    out_s,
    heads,
    send,
    recv,
    local_sem,
):
    links = Links(send, recv)
    x, y, core = links.x, links.y, links.core
    others = [(dy, dc) for dy in range(4) for dc in range(2) if (dy, dc) != (0, 0)]
    turns = [(dz, dx) for dz in (0, 3, 1, 2) for dx in range(4)]
    greet(
        [links.patch_device(dx, dz) for dz, dx in turns if (dz, dx) != (0, 0)]
        + [links.frame_device(dy, 0, dc) for dy, dc in others]
        + [links.frame_device(0, dz, 0) for dz in (1, 2, 3)]
    )
    held = (held0, held1)
    normed = rms_norm(tokens_ref[...]).astype(BF16)
    for g in range(8):
        slices[g] = normed[g * KEY_ROWS : (g + 1) * KEY_ROWS]
    picks = []
    for dy, dc in others:
        there = turn(y, dy) * 2 + lax.rem(core + dc, 2)
        slot = (4 - dy) % 4 * 2 + dc
        picks.append(
            links.copy(slices.at[there], first.at[slot], links.frame_device(dy, 0, dc))
        )
    for c in range(CHUNKS):
        held[c][0, 0] = normed[c * ROWS : (c + 1) * ROWS]
    gathers = [Gather(links, held[c], ROWS) for c in range(CHUNKS)]
    gathers[0].begin_z()
    for one in gathers:
        one.send_x(0)
    mine = wt_ref.at[pl.ds(pl.multiple_of((core * 4 + y) * FRAGMENT, 16), FRAGMENT)]
    place = wt.at[links.patch, core, y]
    own = pltpu.make_async_copy(mine, place, local_sem)
    own.start()
    first[0] = slices[y * 2 + core]
    for made in picks:
        made.wait_recv()
    second[0] = first[pick_ref[0]]
    picks = [
        links.copy(second.at[0], second.at[4 - dz], links.frame_device(0, dz, 0))
        for dz in (1, 2, 3)
    ]
    gathers[1].begin_z()
    w[...] = jnp.zeros_like(w)
    for i in range(3):
        w[:, i * LANES : i * LANES + HEAD_DIM] = w_ref[:, i * HEAD_DIM : (i + 1) * HEAD_DIM]
    for one in gathers:
        one.forward_x(0)
    gathers[0].neighbours()
    for made in picks:
        made.wait_recv()
    kheld[0, 0] = second[pick_ref[1]]
    keys = Gather(links, kheld, KEY_ROWS)
    keys.begin_z()
    keys.send_x(0)
    gathers[1].neighbours()
    wt_up = links.copy(mine, place, links.patch_device(0, 1))
    wt_down = links.copy(mine, place, links.patch_device(0, 3))
    keys.neighbours()
    keys.forward_x(0)

    def finish(dz):
        for c in range(CHUNKS):
            gathers[c].done_x(dz)
            out = jnp.dot(
                held[c][dz].reshape(4 * ROWS, D), w[...], preferred_element_type=F32
            )
            q = (out[:, :LANES] * (HEAD_DIM**-0.5 * LOG2E)).astype(BF16)
            for dx in range(4):
                at = (dz * 4 + dx) * BLOCK + c * ROWS
                q_s[at : at + ROWS, :] = q[dx * ROWS : (dx + 1) * ROWS]
            at = (dz * CHUNKS + c) * 4 * ROWS
            kt[:, at : at + 4 * ROWS] = out[:, LANES : 2 * LANES].T.astype(BF16)
            v_s[at : at + 4 * ROWS, :] = with_ones(out[:, 2 * LANES :]).astype(BF16)

    finish(0)
    for dz in (3, 1):
        for one in (gathers[0], gathers[1]):
            one.forward_x(dz)
    for one in (gathers[0], gathers[1]):
        one.opposite()
    for dz in (3, 1):
        keys.forward_x(dz)
    keys.opposite()
    wt_up.wait_recv()
    below = wt.at[x * 4 + turn(links.zh, 3), core, y]
    wt_far = links.copy(below, below, links.patch_device(0, 1))
    finish(3)
    finish(1)
    for one in (gathers[0], gathers[1], keys):
        one.forward_x(2)
    own.wait()
    wt_down.wait_recv()
    wt_far.wait_recv()
    group = pl.ds(x * 4, 4)
    upper, lower = pl.ds(0, SPLIT), pl.ds(SPLIT, FRAGMENT - SPLIT)
    by_y, by_x = wt.at[group, core, y, upper], wt.at[group, core, y, lower]
    for dz in range(4):
        keys.done_x(dz)
    kv_out[...] = jnp.dot(
        kheld[...].reshape(16 * KEY_ROWS, D), w[:, LANES:], preferred_element_type=F32
    ).astype(BF16)
    twin = links.frame_device(0, 0, 1)
    kv_y = [
        (links.copy(kv_out, kv_in.at[(4 - d) * 2], links.frame_device(d, 0, 0)), (4 - d) * 2)
        for d in (1, 3, 2)
    ]
    kv_twin = [links.copy(kv_out, kv_in.at[1], twin)]
    steps = []
    for d in (1, 3, 2):
        steps.append(links.copy(by_y, by_y, links.frame_device(d, 0, 0)))
        steps.append(links.copy(by_x, by_x, links.patch_device(d, 0)))
    finish(2)
    for made in steps:
        made.wait_recv()
    def along_x(dx, rows=upper, half=slice(0, 4)):
        return wt.at[pl.ds(turn(x, dx) * 4, 4), core, pl.ds(half.start, half.stop - half.start), rows]

    def along_y(dy, half=slice(0, 16)):
        return wt.at[pl.ds(half.start, half.stop - half.start), core, turn(y, dy), lower]

    def pass_on(piece, device):
        return links.copy(piece, piece, device)

    x_up = pass_on(along_x(0), links.patch_device(1, 0))
    x_down = pass_on(along_x(0), links.patch_device(3, 0))
    y_up = pass_on(along_y(0), links.frame_device(1, 0, 0))
    y_down = pass_on(along_y(0), links.frame_device(3, 0, 0))
    cross = [pass_on(along_x(0), twin), pass_on(along_y(0), twin)]

    def scores_of(g, keys):
        q = q_s[g * GROUP : (g + 1) * GROUP, :]
        scores = jnp.dot(q, kt[:, keys], preferred_element_type=F32)
        return scores, jnp.max(scores, axis=-1, keepdims=True)

    for g in range(4):
        scores, largest = scores_of(g, slice(0, PATCHES))
        weights = jnp.exp2(scores - largest).astype(BF16)
        total_s[g] = jnp.dot(weights, v_s[:PATCHES, :], preferred_element_type=F32)
        largest_s[g] = jnp.broadcast_to(largest, (GROUP, LANES))
        if g == 0:
            for made, slot in kv_y:
                made.wait_recv()
                kv_twin.append(links.copy(kv_in.at[slot], kv_in.at[slot + 1], twin))
    kv_in[0] = kv_out[...]
    for made in kv_twin:
        made.wait_recv()
    for g in range(8):
        at = PATCHES + g * 16 * KEY_ROWS
        kt[:, at : at + 16 * KEY_ROWS] = kv_in[g, :, :LANES].T
        v_s[at : at + 16 * KEY_ROWS, :] = with_ones(kv_in[g, :, LANES:].astype(F32)).astype(BF16)
    sent = []
    for i, g in enumerate((2, 3, 1, 0)):
        scores, new = scores_of(g, slice(PATCHES, 2 * PATCHES))
        largest = largest_s[g][:, :1]
        new = jnp.maximum(largest, new)
        weights = jnp.exp2(scores - new).astype(BF16)
        total = total_s[g] * jnp.exp2(largest - new) + jnp.dot(
            weights, v_s[PATCHES:, :], preferred_element_type=F32
        )
        turned = (total / total[:, HEAD_DIM : HEAD_DIM + 1]).T
        for dx in (2, 1, 3, 0):
            block = turned[:HEAD_DIM, dx * BLOCK : (dx + 1) * BLOCK].astype(BF16)
            if (g, dx) == (0, 0):
                heads[links.patch] = block
            else:
                out_s[g * 4 + dx] = block
                sent.append(
                    links.copy(
                        out_s.at[g * 4 + dx], heads.at[links.patch], links.patch_device(dx, g)
                    )
                )
        if i == 1:
            x_up.wait_recv()
            far = [pass_on(along_x(3, half=slice(0, 2)), links.patch_device(1, 0))]
            cross.append(pass_on(along_x(3), twin))
            y_up.wait_recv()
            far.append(pass_on(along_y(3, slice(0, 8)), links.frame_device(1, 0, 0)))
            cross.append(pass_on(along_y(3), twin))
            x_down.wait_recv()
            far.append(pass_on(along_x(1, half=slice(2, 4)), links.patch_device(3, 0)))
            cross.append(pass_on(along_x(1), twin))
            y_down.wait_recv()
            far.append(pass_on(along_y(1, slice(8, 16)), links.frame_device(3, 0, 0)))
            cross.append(pass_on(along_y(1), twin))
    for made in sent:
        made.wait_recv()
    rows = heads[...].reshape(D, BLOCK).T
    spatial = jnp.dot(rows, out_w_ref[...], preferred_element_type=F32).astype(BF16)
    spatial_ref[...] = spatial
    normed_ref[...] = rms_norm(spatial).astype(BF16)
    for made in far:
        made.wait_recv()
    cross.append(pass_on(along_x(2), twin))
    cross.append(pass_on(along_y(2), twin))
    for made in cross:
        made.wait_recv()
    links.finish()


def spatial_branch(pick, tokens, w, wt, out_w):
    vmem = pl.BlockSpec(memory_space=pltpu.VMEM)
    anywhere = pl.BlockSpec(memory_space=pl.ANY)
    columns = wt.shape[1]
    return pl.pallas_call(
        spatial_kernel,
        out_shape=[
            jax.ShapeDtypeStruct((BLOCK, D), BF16),
            jax.ShapeDtypeStruct((BLOCK, D), BF16),
            jax.ShapeDtypeStruct((HEADS, 2, 4, FRAGMENT, columns), BF16),
        ],
        in_specs=[pl.BlockSpec(memory_space=pltpu.SMEM), vmem, vmem, anywhere, vmem],
        out_specs=[vmem, vmem, anywhere],
        scratch_shapes=[
            pltpu.VMEM((4, 4, ROWS, D), BF16),
            pltpu.VMEM((4, 4, ROWS, D), BF16),
            pltpu.VMEM((4, 4, KEY_ROWS, D), BF16),
            pltpu.VMEM((8, KEY_ROWS, D), BF16),
            pltpu.VMEM((8, KEY_ROWS, D), BF16),
            pltpu.VMEM((4, KEY_ROWS, D), BF16),
            pltpu.VMEM((D, 3 * LANES), BF16),
            pltpu.VMEM((PATCHES, LANES), BF16),
            pltpu.VMEM((LANES, 2 * PATCHES), BF16),
            pltpu.VMEM((2 * PATCHES, LANES), BF16),
            pltpu.VMEM((16 * KEY_ROWS, 2 * LANES), BF16),
            pltpu.VMEM((8, 16 * KEY_ROWS, 2 * LANES), BF16),
            pltpu.VMEM((4, GROUP, LANES), F32),
            pltpu.VMEM((4, GROUP, LANES), F32),
            pltpu.VMEM((HEADS, HEAD_DIM, BLOCK), BF16),
            pltpu.VMEM((HEADS, HEAD_DIM, BLOCK), BF16),
            pltpu.SemaphoreType.DMA((COPIES,)),
            pltpu.SemaphoreType.DMA((COPIES,)),
            pltpu.SemaphoreType.DMA,
        ],
        compiler_params=pltpu.CompilerParams(
            collective_id=1, has_side_effects=True, vmem_limit_bytes=50 * 2**20
        ),
        name="spatial_branch",
    )(pick, tokens, w, wt, out_w)


HEAD_STEP = 4


def temporal_kernel(x_ref, wt_ref, o_ref, turned):
    step = pl.program_id(0)
    x = x_ref[...]
    row = lax.broadcasted_iota(jnp.int32, (BLOCK, BLOCK), 0)
    column = lax.broadcasted_iota(jnp.int32, (BLOCK, BLOCK), 1)
    same = (row & 3) == (column & 3)
    for h in range(HEAD_STEP):
        w = wt_ref[h].reshape(D, 3 * HEAD_DIM)
        qkv = jnp.dot(x, w, preferred_element_type=F32).astype(BF16)
        q, k = qkv[:, :HEAD_DIM], qkv[:, HEAD_DIM : 2 * HEAD_DIM]
        scores = lax.dot_general(
            q, k, (((1,), (1,)), ((), ())), preferred_element_type=F32
        ) * (HEAD_DIM**-0.5)
        scores = jnp.where(same, scores, -jnp.inf)
        exponent = jnp.exp(scores - jnp.max(scores, axis=-1, keepdims=True))
        weights = (exponent / jnp.sum(exponent, axis=-1, keepdims=True)).astype(BF16)
        out = jnp.dot(weights, qkv, preferred_element_type=F32)
        turned[step * HEAD_STEP + h] = out.T[2 * HEAD_DIM :, :]

    @pl.when(step == HEADS // HEAD_STEP - 1)
    def _():
        o_ref[...] = turned[...].reshape(D, BLOCK).T.astype(BF16)


def temporal_attend(x, wt):
    whole = pl.BlockSpec((BLOCK, D), lambda i: (0, 0))
    return pl.pallas_call(
        temporal_kernel,
        grid=(HEADS // HEAD_STEP,),
        out_shape=jax.ShapeDtypeStruct((BLOCK, D), BF16),
        in_specs=[
            whole,
            pl.BlockSpec((HEAD_STEP,) + wt.shape[1:], lambda i: (i, 0, 0, 0, 0)),
        ],
        out_specs=whole,
        scratch_shapes=[pltpu.VMEM((HEADS, HEAD_DIM, BLOCK), F32)],
        compiler_params=pltpu.CompilerParams(vmem_limit_bytes=48 * 2**20),
        name="temporal_attend",
    )(x, wt)


def per_device(tokens, key_frame, qkv_spatial, out_spatial, qkv_temporal):
    frame = lax.axis_index("frame")
    key = key_frame[0].astype(jnp.int32)
    y, zl, core = frame // 8, (frame // 2) % 4, frame % 2
    pick = jnp.stack(
        [(key // 8 - y) % 4 * 2 + (key % 2 - core) % 2, (key // 2 % 4 - zl) % 4]
    ).astype(jnp.int32)
    spatial, temporal_in, wt = spatial_branch(
        pick, tokens[0], qkv_spatial, qkv_temporal, out_spatial
    )
    rows = lax.all_to_all(
        temporal_in.reshape(32, 4, D), "frame", split_axis=0, concat_axis=0, tiled=True
    )
    mixed = temporal_attend(rows.reshape(BLOCK, D), wt)
    temporal = lax.all_to_all(
        mixed.reshape(32, 4, D), "frame", split_axis=0, concat_axis=0, tiled=True
    )
    return (spatial[None], temporal.reshape(1, BLOCK, D))


def solution(mesh):
    return jax.shard_map(
        per_device,
        mesh=mesh,
        in_specs=(P("frame", "patch", None), P(), P(None, "patch"), P(), P(None, "patch")),
        out_specs=(P("frame", "patch", None), P("frame", "patch", None)),
        check_vma=False,
    )
```

```python
import functools

import jax
import jax.numpy as jnp
from jax import lax
from jax.experimental import pallas as pl
from jax.experimental.pallas import tpu as pltpu
from jax.sharding import PartitionSpec as P

D = 1152
HEADS = 16
HEAD_DIM = 72
PATCHES = 2048
FRAMES = 32
BLOCK = 128
GROUP_ROWS = BLOCK // FRAMES
LANES = 128
CHUNKS = 2
ROWS = BLOCK // CHUNKS
KEY_ROWS = 16
FRAGMENT = D // 8
epsilon = 1e-06
LOG2E = 1.4426950408889634
BF16 = jnp.bfloat16
F32 = jnp.float32


def rms_norm(values):
    values = values.astype(F32)
    return values * lax.rsqrt(jnp.mean(values * values, axis=-1, keepdims=True) + epsilon)


def places():
    patch, frame = lax.axis_index("patch"), lax.axis_index("frame")
    return (
        patch,
        frame,
        lax.div(patch, 4),
        lax.rem(patch, 4),
        lax.div(frame, 8),
        lax.rem(lax.div(frame, 2), 4),
        lax.rem(frame, 2),
    )


def turn(at, by):
    return lax.rem(at + by, 4)


class Links:
    def __init__(self, send, recv):
        self.send, self.recv, self.used, self.open = send, recv, 0, []
        self.patch, self.frame, self.x, self.zh, self.y, self.zl, self.core = places()

    def patch_device(self, dx, dz):
        return (self.frame, turn(self.x, dx) * 4 + turn(self.zh, dz))

    def frame_device(self, dy, dz, dc):
        frame = turn(self.y, dy) * 8 + turn(self.zl, dz) * 2 + lax.rem(self.core + dc, 2)
        return (frame, self.patch)

    def frame_at(self, by):
        return (lax.rem(self.frame + by, FRAMES), self.patch)

    def copy(self, src, dst, device):
        made = pltpu.make_async_remote_copy(
            src_ref=src,
            dst_ref=dst,
            send_sem=self.send.at[self.used],
            recv_sem=self.recv.at[self.used],
            device_id=device,
            device_id_type=pl.DeviceIdType.MESH,
        )
        made.start()
        self.used += 1
        self.open.append(made)
        return made

    def finish(self):
        for made in self.open:
            made.wait_send()


def greet(devices):
    barrier = pltpu.get_barrier_semaphore()
    for device in devices:
        pl.semaphore_signal(barrier, inc=1, device_id=device, device_id_type=pl.DeviceIdType.MESH)
    pl.semaphore_wait(barrier, len(devices))


class Gather:
    def __init__(self, links, held, rows):
        self.links, self.held, self.rows = links, held, rows
        self.along_x = {}
        self.last = {}

    def halves(self):
        if self.rows % 32:
            return [(pl.ds(0, self.rows), 0)]
        half = self.rows // 2
        return [(pl.ds(0, half), 0), (pl.ds(half, half), 1)]

    def send_x(self, dz):
        links, held = self.links, self.held
        self.along_x[dz] = (
            links.copy(held.at[dz, 0], held.at[dz, 3], links.patch_device(1, 0)),
            links.copy(held.at[dz, 0], held.at[dz, 1], links.patch_device(3, 0)),
        )

    def begin_z(self):
        links, held = self.links, self.held
        self.up = links.copy(held.at[0, 0], held.at[3, 0], links.patch_device(0, 1))
        self.down = links.copy(held.at[0, 0], held.at[1, 0], links.patch_device(0, 3))

    def neighbours(self):
        links, held = self.links, self.held
        self.far = []
        self.up.wait_recv()
        for part, way in self.halves():
            if way == 0:
                self.far.append(
                    links.copy(held.at[3, 0, part], held.at[2, 0, part], links.patch_device(0, 1))
                )
        self.send_x(3)
        self.down.wait_recv()
        for part, way in self.halves():
            if way == 1:
                self.far.append(
                    links.copy(held.at[1, 0, part], held.at[2, 0, part], links.patch_device(0, 3))
                )
        self.send_x(1)

    def opposite(self):
        for made in self.far:
            made.wait_recv()
        self.send_x(2)

    def forward_x(self, dz):
        links, held = self.links, self.held
        up, down = self.along_x[dz]
        self.last[dz] = []
        up.wait_recv()
        for part, way in self.halves():
            if way == 0:
                self.last[dz].append(
                    links.copy(held.at[dz, 3, part], held.at[dz, 2, part], links.patch_device(1, 0))
                )
        down.wait_recv()
        for part, way in self.halves():
            if way == 1:
                self.last[dz].append(
                    links.copy(held.at[dz, 1, part], held.at[dz, 2, part], links.patch_device(3, 0))
                )

    def done_x(self, dz):
        for made in self.last[dz]:
            made.wait_recv()


def with_ones(values):
    lane = lax.broadcasted_iota(jnp.int32, values.shape, 1)
    return jnp.where(lane == HEAD_DIM, jnp.ones_like(values), values)


GATHER_COPIES = 20
COPIES = (CHUNKS + 1) * GATHER_COPIES + 7 + 3 + 7 + 3 + 6 + 6 + 8 + 15 + 62
SPLIT = 64
GROUP = 512


HEAD_STEP = 4


def scatter(links, values, out, landing):
    for f in range(FRAMES):
        out[f] = values[f * GROUP_ROWS : (f + 1) * GROUP_ROWS].astype(BF16)
    links.slots = [
        links.copy(
            out.at[lax.rem(links.frame + k, FRAMES)], landing.at[links.frame], links.frame_at(k)
        )
        for k in range(1, FRAMES)
    ]
    landing[links.frame] = out[links.frame]


def collect(links, landing, flat):
    for made in links.slots:
        made.wait_recv()
    for f in range(FRAMES):
        flat[f * GROUP_ROWS : (f + 1) * GROUP_ROWS, :] = landing[f].astype(F32)


def mix(rows, wt, turned, first):
    row = lax.broadcasted_iota(jnp.int32, (BLOCK, BLOCK), 0)
    column = lax.broadcasted_iota(jnp.int32, (BLOCK, BLOCK), 1)
    same = lax.rem(row, GROUP_ROWS) == lax.rem(column, GROUP_ROWS)
    heads = range(first, first + HEAD_STEP)
    qkv = [
        jnp.dot(
            rows, wt[h].reshape(D, 3 * HEAD_DIM), preferred_element_type=F32
        ).astype(BF16)
        for h in heads
    ]
    scores = [
        lax.dot_general(
            one[:, :HEAD_DIM],
            one[:, HEAD_DIM : 2 * HEAD_DIM],
            (((1,), (1,)), ((), ())),
            preferred_element_type=F32,
        )
        * (HEAD_DIM**-0.5)
        for one in qkv
    ]
    scores = [jnp.where(same, one, -jnp.inf) for one in scores]
    largest = [jnp.max(one, axis=-1, keepdims=True) for one in scores]
    exponent = [jnp.exp(one - top) for one, top in zip(scores, largest)]
    sums = [jnp.sum(one, axis=-1, keepdims=True) for one in exponent]
    weights = [(one / total).astype(BF16) for one, total in zip(exponent, sums)]
    outs = [
        jnp.dot(one, values, preferred_element_type=F32) for one, values in zip(weights, qkv)
    ]
    for h, out in zip(heads, outs):
        turned[h] = out.T[2 * HEAD_DIM :, :]


def block_kernel(
    pick_ref,
    tokens_ref,
    w_ref,
    wt_ref,
    out_w_ref,
    spatial_ref,
    temporal_ref,
    wt,
    held0,
    held1,
    kheld,
    slices,
    first,
    second,
    w,
    q_s,
    kt,
    v_s,
    kv_out,
    kv_in,
    total_s,
    largest_s,
    out_s,
    heads,
    rows_out,
    rows_in,
    mixed_out,
    mixed_in,
    flat,
    head_rows,
    send,
    recv,
    local_sem,
):
    links = Links(send, recv)
    x, y, core = links.x, links.y, links.core
    others = [(dy, dc) for dy in range(4) for dc in range(2) if (dy, dc) != (0, 0)]
    turns = [(dz, dx) for dz in (0, 3, 1, 2) for dx in range(4)]
    greet(
        [links.patch_device(dx, dz) for dz, dx in turns if (dz, dx) != (0, 0)]
        + [links.frame_at(k) for k in range(1, FRAMES)]
    )
    held = (held0, held1)
    normed = rms_norm(tokens_ref[...]).astype(BF16)
    for g in range(8):
        slices[g] = normed[g * KEY_ROWS : (g + 1) * KEY_ROWS]
    picks = []
    for dy, dc in others:
        there = turn(y, dy) * 2 + lax.rem(core + dc, 2)
        slot = (4 - dy) % 4 * 2 + dc
        picks.append(
            links.copy(slices.at[there], first.at[slot], links.frame_device(dy, 0, dc))
        )
    for c in range(CHUNKS):
        held[c][0, 0] = normed[c * ROWS : (c + 1) * ROWS]
    gathers = [Gather(links, held[c], ROWS) for c in range(CHUNKS)]
    gathers[0].begin_z()
    for one in gathers:
        one.send_x(0)
    mine = wt_ref.at[pl.ds(pl.multiple_of((core * 4 + y) * FRAGMENT, 16), FRAGMENT)]
    place = wt.at[links.patch, core, y]
    own = pltpu.make_async_copy(mine, place, local_sem)
    own.start()
    first[0] = slices[y * 2 + core]
    for made in picks:
        made.wait_recv()
    second[0] = first[pick_ref[0]]
    picks = [
        links.copy(second.at[0], second.at[4 - dz], links.frame_device(0, dz, 0))
        for dz in (1, 2, 3)
    ]
    gathers[1].begin_z()
    w[...] = jnp.zeros_like(w)
    for i in range(3):
        w[:, i * LANES : i * LANES + HEAD_DIM] = w_ref[:, i * HEAD_DIM : (i + 1) * HEAD_DIM]
    for one in gathers:
        one.forward_x(0)
    gathers[0].neighbours()
    for made in picks:
        made.wait_recv()
    kheld[0, 0] = second[pick_ref[1]]
    keys = Gather(links, kheld, KEY_ROWS)
    keys.begin_z()
    keys.send_x(0)
    gathers[1].neighbours()
    wt_up = links.copy(mine, place, links.patch_device(0, 1))
    wt_down = links.copy(mine, place, links.patch_device(0, 3))
    keys.neighbours()
    keys.forward_x(0)

    def finish(dz):
        for c in range(CHUNKS):
            gathers[c].done_x(dz)
            out = jnp.dot(
                held[c][dz].reshape(4 * ROWS, D), w[...], preferred_element_type=F32
            )
            q = (out[:, :LANES] * (HEAD_DIM**-0.5 * LOG2E)).astype(BF16)
            for dx in range(4):
                at = (dz * 4 + dx) * BLOCK + c * ROWS
                q_s[at : at + ROWS, :] = q[dx * ROWS : (dx + 1) * ROWS]
            at = (dz * CHUNKS + c) * 4 * ROWS
            kt[:, at : at + 4 * ROWS] = out[:, LANES : 2 * LANES].T.astype(BF16)
            v_s[at : at + 4 * ROWS, :] = with_ones(out[:, 2 * LANES :]).astype(BF16)

    finish(0)
    for dz in (3, 1):
        for one in (gathers[0], gathers[1]):
            one.forward_x(dz)
    for one in (gathers[0], gathers[1]):
        one.opposite()
    for dz in (3, 1):
        keys.forward_x(dz)
    keys.opposite()
    wt_up.wait_recv()
    below = wt.at[x * 4 + turn(links.zh, 3), core, y]
    wt_far = links.copy(below, below, links.patch_device(0, 1))
    finish(3)
    finish(1)
    for one in (gathers[0], gathers[1], keys):
        one.forward_x(2)
    own.wait()
    wt_down.wait_recv()
    wt_far.wait_recv()
    group = pl.ds(x * 4, 4)
    upper, lower = pl.ds(0, SPLIT), pl.ds(SPLIT, FRAGMENT - SPLIT)
    by_y, by_x = wt.at[group, core, y, upper], wt.at[group, core, y, lower]
    for dz in range(4):
        keys.done_x(dz)
    kv_out[...] = jnp.dot(
        kheld[...].reshape(16 * KEY_ROWS, D), w[:, LANES:], preferred_element_type=F32
    ).astype(BF16)
    twin = links.frame_device(0, 0, 1)
    kv_y = [
        (links.copy(kv_out, kv_in.at[(4 - d) * 2], links.frame_device(d, 0, 0)), (4 - d) * 2)
        for d in (1, 3, 2)
    ]
    kv_twin = [links.copy(kv_out, kv_in.at[1], twin)]
    steps = []
    for d in (1, 3, 2):
        steps.append(links.copy(by_y, by_y, links.frame_device(d, 0, 0)))
        steps.append(links.copy(by_x, by_x, links.patch_device(d, 0)))
    finish(2)
    for made in steps:
        made.wait_recv()
    def along_x(dx, rows=upper, half=slice(0, 4)):
        return wt.at[pl.ds(turn(x, dx) * 4, 4), core, pl.ds(half.start, half.stop - half.start), rows]

    def along_y(dy, half=slice(0, 16)):
        return wt.at[pl.ds(half.start, half.stop - half.start), core, turn(y, dy), lower]

    def pass_on(piece, device):
        return links.copy(piece, piece, device)

    x_up = pass_on(along_x(0), links.patch_device(1, 0))
    x_down = pass_on(along_x(0), links.patch_device(3, 0))
    y_up = pass_on(along_y(0), links.frame_device(1, 0, 0))
    y_down = pass_on(along_y(0), links.frame_device(3, 0, 0))
    cross = [pass_on(along_x(0), twin), pass_on(along_y(0), twin)]

    def scores_of(g, keys):
        q = q_s[g * GROUP : (g + 1) * GROUP, :]
        scores = jnp.dot(q, kt[:, keys], preferred_element_type=F32)
        return scores, jnp.max(scores, axis=-1, keepdims=True)

    for g in range(4):
        scores, largest = scores_of(g, slice(0, PATCHES))
        weights = jnp.exp2(scores - largest).astype(BF16)
        total_s[g] = jnp.dot(weights, v_s[:PATCHES, :], preferred_element_type=F32)
        largest_s[g] = jnp.broadcast_to(largest, (GROUP, LANES))
        if g == 0:
            for made, slot in kv_y:
                made.wait_recv()
                kv_twin.append(links.copy(kv_in.at[slot], kv_in.at[slot + 1], twin))
    kv_in[0] = kv_out[...]
    for made in kv_twin:
        made.wait_recv()
    for g in range(8):
        at = PATCHES + g * 16 * KEY_ROWS
        kt[:, at : at + 16 * KEY_ROWS] = kv_in[g, :, :LANES].T
        v_s[at : at + 16 * KEY_ROWS, :] = with_ones(kv_in[g, :, LANES:].astype(F32)).astype(BF16)
    sent = []
    for g in (2, 3, 1, 0):
        scores, new = scores_of(g, slice(PATCHES, 2 * PATCHES))
        largest = largest_s[g][:, :1]
        new = jnp.maximum(largest, new)
        weights = jnp.exp2(scores - new).astype(BF16)
        total = total_s[g] * jnp.exp2(largest - new) + jnp.dot(
            weights, v_s[PATCHES:, :], preferred_element_type=F32
        )
        turned = (total / total[:, HEAD_DIM : HEAD_DIM + 1]).T
        for dx in (2, 1, 3, 0):
            block = turned[:HEAD_DIM, dx * BLOCK : (dx + 1) * BLOCK].astype(BF16)
            if (g, dx) == (0, 0):
                heads[links.patch] = block
            else:
                out_s[g * 4 + dx] = block
                sent.append(
                    links.copy(
                        out_s.at[g * 4 + dx], heads.at[links.patch], links.patch_device(dx, g)
                    )
                )
    x_up.wait_recv()
    far = [pass_on(along_x(3, half=slice(0, 2)), links.patch_device(1, 0))]
    cross.append(pass_on(along_x(3), twin))
    y_up.wait_recv()
    far.append(pass_on(along_y(3, slice(0, 8)), links.frame_device(1, 0, 0)))
    cross.append(pass_on(along_y(3), twin))
    x_down.wait_recv()
    far.append(pass_on(along_x(1, half=slice(2, 4)), links.patch_device(3, 0)))
    cross.append(pass_on(along_x(1), twin))
    y_down.wait_recv()
    far.append(pass_on(along_y(1, slice(8, 16)), links.frame_device(3, 0, 0)))
    cross.append(pass_on(along_y(1), twin))
    for made in sent:
        made.wait_recv()
    rows = heads[...].reshape(D, BLOCK).T
    spatial = jnp.dot(rows, out_w_ref[...], preferred_element_type=F32).astype(BF16)
    spatial_ref[...] = spatial
    scatter(links, rms_norm(spatial), rows_out, rows_in)
    for made in far:
        made.wait_recv()
    cross.append(pass_on(along_x(2), twin))
    cross.append(pass_on(along_y(2), twin))
    collect(links, rows_in, flat)
    rows = flat[...].astype(BF16)
    for made in cross:
        made.wait_recv()
    for h in range(0, HEADS, HEAD_STEP):
        mix(rows, wt, head_rows, h)
    scatter(links, head_rows[...].reshape(D, BLOCK).T, mixed_out, mixed_in)
    collect(links, mixed_in, flat)
    temporal_ref[...] = flat[...].astype(BF16)
    links.finish()


def block(pick, tokens, w, wt, out_w):
    vmem = pl.BlockSpec(memory_space=pltpu.VMEM)
    anywhere = pl.BlockSpec(memory_space=pl.ANY)
    columns = wt.shape[1]
    return pl.pallas_call(
        block_kernel,
        out_shape=[
            jax.ShapeDtypeStruct((BLOCK, D), BF16),
            jax.ShapeDtypeStruct((BLOCK, D), BF16),
        ],
        in_specs=[pl.BlockSpec(memory_space=pltpu.SMEM), vmem, vmem, anywhere, vmem],
        out_specs=[vmem, vmem],
        scratch_shapes=[
            pltpu.VMEM((HEADS, 2, 4, FRAGMENT, columns), BF16),
            pltpu.VMEM((4, 4, ROWS, D), BF16),
            pltpu.VMEM((4, 4, ROWS, D), BF16),
            pltpu.VMEM((4, 4, KEY_ROWS, D), BF16),
            pltpu.VMEM((8, KEY_ROWS, D), BF16),
            pltpu.VMEM((8, KEY_ROWS, D), BF16),
            pltpu.VMEM((4, KEY_ROWS, D), BF16),
            pltpu.VMEM((D, 3 * LANES), BF16),
            pltpu.VMEM((PATCHES, LANES), BF16),
            pltpu.VMEM((LANES, 2 * PATCHES), BF16),
            pltpu.VMEM((2 * PATCHES, LANES), BF16),
            pltpu.VMEM((16 * KEY_ROWS, 2 * LANES), BF16),
            pltpu.VMEM((8, 16 * KEY_ROWS, 2 * LANES), BF16),
            pltpu.VMEM((4, GROUP, LANES), F32),
            pltpu.VMEM((4, GROUP, LANES), F32),
            pltpu.VMEM((HEADS, HEAD_DIM, BLOCK), BF16),
            pltpu.VMEM((HEADS, HEAD_DIM, BLOCK), BF16),
            pltpu.VMEM((FRAMES, GROUP_ROWS, D), BF16),
            pltpu.VMEM((FRAMES, GROUP_ROWS, D), BF16),
            pltpu.VMEM((FRAMES, GROUP_ROWS, D), BF16),
            pltpu.VMEM((FRAMES, GROUP_ROWS, D), BF16),
            pltpu.VMEM((BLOCK, D), F32),
            pltpu.VMEM((HEADS, HEAD_DIM, BLOCK), F32),
            pltpu.SemaphoreType.DMA((COPIES,)),
            pltpu.SemaphoreType.DMA((COPIES,)),
            pltpu.SemaphoreType.DMA,
        ],
        compiler_params=pltpu.CompilerParams(
            collective_id=1, has_side_effects=True, vmem_limit_bytes=50 * 2**20
        ),
        name="block",
    )(pick, tokens, w, wt, out_w)


def per_device(tokens, key_frame, qkv_spatial, out_spatial, qkv_temporal):
    frame = lax.axis_index("frame")
    key = key_frame[0].astype(jnp.int32)
    y, zl, core = frame // 8, (frame // 2) % 4, frame % 2
    pick = jnp.stack(
        [(key // 8 - y) % 4 * 2 + (key % 2 - core) % 2, (key // 2 % 4 - zl) % 4]
    ).astype(jnp.int32)
    spatial, temporal = block(
        pick, tokens[0], qkv_spatial, qkv_temporal, out_spatial
    )
    return (spatial[None], temporal[None])


def solution(mesh):
    return jax.shard_map(
        per_device,
        mesh=mesh,
        in_specs=(P("frame", "patch", None), P(), P(None, "patch"), P(), P(None, "patch")),
        out_specs=(P("frame", "patch", None), P("frame", "patch", None)),
        check_vma=False,
    )
```

```python
import functools

import jax
import jax.numpy as jnp
from jax import lax
from jax.experimental import pallas as pl
from jax.experimental.pallas import tpu as pltpu
from jax.sharding import PartitionSpec as P

D = 1152
HEADS = 16
HEAD_DIM = 72
PATCHES = 2048
FRAMES = 32
BLOCK = 128
GROUP_ROWS = BLOCK // FRAMES
LANES = 128
CHUNKS = 2
ROWS = BLOCK // CHUNKS
KEY_ROWS = 16
FRAGMENT = D // 8
epsilon = 1e-06
LOG2E = 1.4426950408889634
BF16 = jnp.bfloat16
F32 = jnp.float32


def rms_norm(values):
    values = values.astype(F32)
    return values * lax.rsqrt(jnp.mean(values * values, axis=-1, keepdims=True) + epsilon)


def places():
    patch, frame = lax.axis_index("patch"), lax.axis_index("frame")
    return (
        patch,
        frame,
        lax.div(patch, 4),
        lax.rem(patch, 4),
        lax.div(frame, 8),
        lax.rem(lax.div(frame, 2), 4),
        lax.rem(frame, 2),
    )


def turn(at, by):
    return lax.rem(at + by, 4)


class Links:
    def __init__(self, send, recv):
        self.send, self.recv, self.used, self.open = send, recv, 0, []
        self.patch, self.frame, self.x, self.zh, self.y, self.zl, self.core = places()

    def patch_device(self, dx, dz):
        return (self.frame, turn(self.x, dx) * 4 + turn(self.zh, dz))

    def frame_device(self, dy, dz, dc):
        frame = turn(self.y, dy) * 8 + turn(self.zl, dz) * 2 + lax.rem(self.core + dc, 2)
        return (frame, self.patch)

    def frame_at(self, by):
        return (lax.rem(self.frame + by, FRAMES), self.patch)

    def copy(self, src, dst, device):
        made = pltpu.make_async_remote_copy(
            src_ref=src,
            dst_ref=dst,
            send_sem=self.send.at[self.used],
            recv_sem=self.recv.at[self.used],
            device_id=device,
            device_id_type=pl.DeviceIdType.MESH,
        )
        made.start()
        self.used += 1
        self.open.append(made)
        return made

    def finish(self):
        for made in self.open:
            made.wait_send()


def greet(devices):
    barrier = pltpu.get_barrier_semaphore()
    for device in devices:
        pl.semaphore_signal(barrier, inc=1, device_id=device, device_id_type=pl.DeviceIdType.MESH)
    pl.semaphore_wait(barrier, len(devices))


class Gather:
    def __init__(self, links, held, rows):
        self.links, self.held, self.rows = links, held, rows
        self.along_x = {}
        self.last = {}

    def halves(self):
        if self.rows % 32:
            return [(pl.ds(0, self.rows), 0)]
        half = self.rows // 2
        return [(pl.ds(0, half), 0), (pl.ds(half, half), 1)]

    def send_x(self, dz):
        links, held = self.links, self.held
        self.along_x[dz] = (
            links.copy(held.at[dz, 0], held.at[dz, 3], links.patch_device(1, 0)),
            links.copy(held.at[dz, 0], held.at[dz, 1], links.patch_device(3, 0)),
        )

    def begin_z(self):
        links, held = self.links, self.held
        self.up = links.copy(held.at[0, 0], held.at[3, 0], links.patch_device(0, 1))
        self.down = links.copy(held.at[0, 0], held.at[1, 0], links.patch_device(0, 3))

    def neighbours(self):
        links, held = self.links, self.held
        self.far = []
        self.up.wait_recv()
        for part, way in self.halves():
            if way == 0:
                self.far.append(
                    links.copy(held.at[3, 0, part], held.at[2, 0, part], links.patch_device(0, 1))
                )
        self.send_x(3)
        self.down.wait_recv()
        for part, way in self.halves():
            if way == 1:
                self.far.append(
                    links.copy(held.at[1, 0, part], held.at[2, 0, part], links.patch_device(0, 3))
                )
        self.send_x(1)

    def opposite(self):
        for made in self.far:
            made.wait_recv()
        self.send_x(2)

    def forward_x(self, dz):
        links, held = self.links, self.held
        up, down = self.along_x[dz]
        self.last[dz] = []
        up.wait_recv()
        for part, way in self.halves():
            if way == 0:
                self.last[dz].append(
                    links.copy(held.at[dz, 3, part], held.at[dz, 2, part], links.patch_device(1, 0))
                )
        down.wait_recv()
        for part, way in self.halves():
            if way == 1:
                self.last[dz].append(
                    links.copy(held.at[dz, 1, part], held.at[dz, 2, part], links.patch_device(3, 0))
                )

    def done_x(self, dz):
        for made in self.last[dz]:
            made.wait_recv()


def with_ones(values):
    lane = lax.broadcasted_iota(jnp.int32, values.shape, 1)
    return jnp.where(lane == HEAD_DIM, jnp.ones_like(values), values)


GATHER_COPIES = 20
COPIES = (CHUNKS + 1) * GATHER_COPIES + 7 + 3 + 7 + 3 + 6 + 6 + 8 + 15 + 62
SPLIT = 64
GROUP = 512


HEAD_STEP = 4


def scatter(links, values, out, landing):
    for f in range(FRAMES):
        out[f] = values[f * GROUP_ROWS : (f + 1) * GROUP_ROWS].astype(BF16)
    links.slots = [
        links.copy(
            out.at[lax.rem(links.frame + k, FRAMES)], landing.at[links.frame], links.frame_at(k)
        )
        for k in range(1, FRAMES)
    ]
    landing[links.frame] = out[links.frame]


def collect(links, landing, flat):
    for made in links.slots:
        made.wait_recv()
    for f in range(FRAMES):
        flat[f * GROUP_ROWS : (f + 1) * GROUP_ROWS, :] = landing[f].astype(F32)


def mix(rows, wt, turned, first):
    row = lax.broadcasted_iota(jnp.int32, (BLOCK, BLOCK), 0)
    column = lax.broadcasted_iota(jnp.int32, (BLOCK, BLOCK), 1)
    same = lax.rem(row, GROUP_ROWS) == lax.rem(column, GROUP_ROWS)
    heads = range(first, first + HEAD_STEP)
    qkv = [
        jnp.dot(
            rows, wt[h].reshape(D, 3 * HEAD_DIM), preferred_element_type=F32
        ).astype(BF16)
        for h in heads
    ]
    scores = [
        lax.dot_general(
            one[:, :HEAD_DIM],
            one[:, HEAD_DIM : 2 * HEAD_DIM],
            (((1,), (1,)), ((), ())),
            preferred_element_type=F32,
        )
        * (HEAD_DIM**-0.5)
        for one in qkv
    ]
    scores = [jnp.where(same, one, -jnp.inf) for one in scores]
    largest = [jnp.max(one, axis=-1, keepdims=True) for one in scores]
    exponent = [jnp.exp(one - top) for one, top in zip(scores, largest)]
    sums = [jnp.sum(one, axis=-1, keepdims=True) for one in exponent]
    weights = [(one / total).astype(BF16) for one, total in zip(exponent, sums)]
    outs = [
        jnp.dot(one, values, preferred_element_type=F32) for one, values in zip(weights, qkv)
    ]
    for h, out in zip(heads, outs):
        turned[h] = out.T[2 * HEAD_DIM :, :]


def block_kernel(
    pick_ref,
    tokens_ref,
    w_ref,
    wt_ref,
    out_w_ref,
    spatial_ref,
    temporal_ref,
    wt,
    held0,
    held1,
    kheld,
    slices,
    first,
    second,
    w,
    q_s,
    kt,
    v_s,
    kv_out,
    kv_in,
    total_s,
    largest_s,
    out_s,
    heads,
    rows_out,
    rows_in,
    mixed_out,
    mixed_in,
    flat,
    head_rows,
    send,
    recv,
    local_sem,
):
    links = Links(send, recv)
    x, y, core = links.x, links.y, links.core
    others = [(dy, dc) for dy in range(4) for dc in range(2) if (dy, dc) != (0, 0)]
    turns = [(dz, dx) for dz in (0, 3, 1, 2) for dx in range(4)]
    greet(
        [links.patch_device(dx, dz) for dz, dx in turns if (dz, dx) != (0, 0)]
        + [links.frame_at(k) for k in range(1, FRAMES)]
    )
    held = (held0, held1)
    normed = rms_norm(tokens_ref[...]).astype(BF16)
    for g in range(8):
        slices[g] = normed[g * KEY_ROWS : (g + 1) * KEY_ROWS]
    picks = []
    for dy, dc in others:
        there = turn(y, dy) * 2 + lax.rem(core + dc, 2)
        slot = (4 - dy) % 4 * 2 + dc
        picks.append(
            links.copy(slices.at[there], first.at[slot], links.frame_device(dy, 0, dc))
        )
    for c in range(CHUNKS):
        held[c][0, 0] = normed[c * ROWS : (c + 1) * ROWS]
    gathers = [Gather(links, held[c], ROWS) for c in range(CHUNKS)]
    gathers[0].begin_z()
    for one in gathers:
        one.send_x(0)
    mine = wt_ref.at[pl.ds(pl.multiple_of((core * 4 + y) * FRAGMENT, 16), FRAGMENT)]
    place = wt.at[links.patch, core, y]
    own = pltpu.make_async_copy(mine, place, local_sem)
    own.start()
    first[0] = slices[y * 2 + core]
    for made in picks:
        made.wait_recv()
    second[0] = first[pick_ref[0]]
    picks = [
        links.copy(second.at[0], second.at[4 - dz], links.frame_device(0, dz, 0))
        for dz in (1, 2, 3)
    ]
    gathers[1].begin_z()
    w[...] = jnp.zeros_like(w)
    for i in range(3):
        w[:, i * LANES : i * LANES + HEAD_DIM] = w_ref[:, i * HEAD_DIM : (i + 1) * HEAD_DIM]
    for one in gathers:
        one.forward_x(0)
    gathers[0].neighbours()
    for made in picks:
        made.wait_recv()
    kheld[0, 0] = second[pick_ref[1]]
    keys = Gather(links, kheld, KEY_ROWS)
    keys.begin_z()
    keys.send_x(0)
    gathers[1].neighbours()
    wt_up = links.copy(mine, place, links.patch_device(0, 1))
    wt_down = links.copy(mine, place, links.patch_device(0, 3))
    keys.neighbours()
    keys.forward_x(0)

    def finish(dz):
        for c in range(CHUNKS):
            gathers[c].done_x(dz)
            out = jnp.dot(
                held[c][dz].reshape(4 * ROWS, D), w[...], preferred_element_type=F32
            )
            q = (out[:, :LANES] * (HEAD_DIM**-0.5 * LOG2E)).astype(BF16)
            for dx in range(4):
                at = (dz * 4 + dx) * BLOCK + c * ROWS
                q_s[at : at + ROWS, :] = q[dx * ROWS : (dx + 1) * ROWS]
            at = (dz * CHUNKS + c) * 4 * ROWS
            kt[:, at : at + 4 * ROWS] = out[:, LANES : 2 * LANES].T.astype(BF16)
            v_s[at : at + 4 * ROWS, :] = with_ones(out[:, 2 * LANES :]).astype(BF16)

    finish(0)
    for dz in (3, 1):
        for one in (gathers[0], gathers[1]):
            one.forward_x(dz)
    for one in (gathers[0], gathers[1]):
        one.opposite()
    for dz in (3, 1):
        keys.forward_x(dz)
    keys.opposite()
    finish(3)
    finish(1)
    for one in (gathers[0], gathers[1], keys):
        one.forward_x(2)
    wt_up.wait_recv()
    below = wt.at[x * 4 + turn(links.zh, 3), core, y]
    wt_far = links.copy(below, below, links.patch_device(0, 1))
    for dz in range(4):
        keys.done_x(dz)
    kv_out[...] = jnp.dot(
        kheld[...].reshape(16 * KEY_ROWS, D), w[:, LANES:], preferred_element_type=F32
    ).astype(BF16)
    twin = links.frame_device(0, 0, 1)
    kv_y = [
        (links.copy(kv_out, kv_in.at[(4 - d) * 2], links.frame_device(d, 0, 0)), (4 - d) * 2)
        for d in (1, 3, 2)
    ]
    kv_twin = [links.copy(kv_out, kv_in.at[1], twin)]
    finish(2)
    own.wait()
    wt_down.wait_recv()
    wt_far.wait_recv()
    group = pl.ds(x * 4, 4)
    upper, lower = pl.ds(0, SPLIT), pl.ds(SPLIT, FRAGMENT - SPLIT)
    by_y, by_x = wt.at[group, core, y, upper], wt.at[group, core, y, lower]
    steps = []
    for d in (1, 3, 2):
        steps.append(links.copy(by_y, by_y, links.frame_device(d, 0, 0)))
        steps.append(links.copy(by_x, by_x, links.patch_device(d, 0)))

    def along_x(dx, rows=upper, half=slice(0, 4)):
        return wt.at[pl.ds(turn(x, dx) * 4, 4), core, pl.ds(half.start, half.stop - half.start), rows]

    def along_y(dy, half=slice(0, 16)):
        return wt.at[pl.ds(half.start, half.stop - half.start), core, turn(y, dy), lower]

    def pass_on(piece, device):
        return links.copy(piece, piece, device)

    def scores_of(g, keys):
        q = q_s[g * GROUP : (g + 1) * GROUP, :]
        scores = jnp.dot(q, kt[:, keys], preferred_element_type=F32)
        return scores, jnp.max(scores, axis=-1, keepdims=True)

    for g in range(4):
        scores, largest = scores_of(g, slice(0, PATCHES))
        weights = jnp.exp2(scores - largest).astype(BF16)
        total_s[g] = jnp.dot(weights, v_s[:PATCHES, :], preferred_element_type=F32)
        largest_s[g] = jnp.broadcast_to(largest, (GROUP, LANES))
        if g == 0:
            for made, slot in kv_y:
                made.wait_recv()
                kv_twin.append(links.copy(kv_in.at[slot], kv_in.at[slot + 1], twin))
    for made in steps:
        made.wait_recv()
    x_up = pass_on(along_x(0), links.patch_device(1, 0))
    x_down = pass_on(along_x(0), links.patch_device(3, 0))
    y_up = pass_on(along_y(0), links.frame_device(1, 0, 0))
    y_down = pass_on(along_y(0), links.frame_device(3, 0, 0))
    cross = [pass_on(along_x(0), twin), pass_on(along_y(0), twin)]
    kv_in[0] = kv_out[...]
    for made in kv_twin:
        made.wait_recv()
    for g in range(8):
        at = PATCHES + g * 16 * KEY_ROWS
        kt[:, at : at + 16 * KEY_ROWS] = kv_in[g, :, :LANES].T
        v_s[at : at + 16 * KEY_ROWS, :] = with_ones(kv_in[g, :, LANES:].astype(F32)).astype(BF16)
    sent = []
    for g in (2, 3, 1, 0):
        scores, new = scores_of(g, slice(PATCHES, 2 * PATCHES))
        largest = largest_s[g][:, :1]
        new = jnp.maximum(largest, new)
        weights = jnp.exp2(scores - new).astype(BF16)
        total = total_s[g] * jnp.exp2(largest - new) + jnp.dot(
            weights, v_s[PATCHES:, :], preferred_element_type=F32
        )
        turned = (total / total[:, HEAD_DIM : HEAD_DIM + 1]).T
        for dx in (2, 1, 3, 0):
            block = turned[:HEAD_DIM, dx * BLOCK : (dx + 1) * BLOCK].astype(BF16)
            if (g, dx) == (0, 0):
                heads[links.patch] = block
            else:
                out_s[g * 4 + dx] = block
                sent.append(
                    links.copy(
                        out_s.at[g * 4 + dx], heads.at[links.patch], links.patch_device(dx, g)
                    )
                )
    for made in sent:
        made.wait_recv()
    rows = heads[...].reshape(D, BLOCK).T
    spatial = jnp.dot(rows, out_w_ref[...], preferred_element_type=F32).astype(BF16)
    spatial_ref[...] = spatial
    scatter(links, rms_norm(spatial), rows_out, rows_in)
    x_up.wait_recv()
    far = [pass_on(along_x(3, half=slice(0, 2)), links.patch_device(1, 0))]
    cross.append(pass_on(along_x(3), twin))
    y_up.wait_recv()
    far.append(pass_on(along_y(3, slice(0, 8)), links.frame_device(1, 0, 0)))
    cross.append(pass_on(along_y(3), twin))
    x_down.wait_recv()
    far.append(pass_on(along_x(1, half=slice(2, 4)), links.patch_device(3, 0)))
    cross.append(pass_on(along_x(1), twin))
    y_down.wait_recv()
    far.append(pass_on(along_y(1, slice(8, 16)), links.frame_device(3, 0, 0)))
    cross.append(pass_on(along_y(1), twin))
    for made in far:
        made.wait_recv()
    cross.append(pass_on(along_x(2), twin))
    cross.append(pass_on(along_y(2), twin))
    collect(links, rows_in, flat)
    rows = flat[...].astype(BF16)
    for made in cross:
        made.wait_recv()
    for h in range(0, HEADS, HEAD_STEP):
        mix(rows, wt, head_rows, h)
    scatter(links, head_rows[...].reshape(D, BLOCK).T, mixed_out, mixed_in)
    collect(links, mixed_in, flat)
    temporal_ref[...] = flat[...].astype(BF16)
    links.finish()


def block(pick, tokens, w, wt, out_w):
    vmem = pl.BlockSpec(memory_space=pltpu.VMEM)
    anywhere = pl.BlockSpec(memory_space=pl.ANY)
    columns = wt.shape[1]
    return pl.pallas_call(
        block_kernel,
        out_shape=[
            jax.ShapeDtypeStruct((BLOCK, D), BF16),
            jax.ShapeDtypeStruct((BLOCK, D), BF16),
        ],
        in_specs=[pl.BlockSpec(memory_space=pltpu.SMEM), vmem, vmem, anywhere, vmem],
        out_specs=[vmem, vmem],
        scratch_shapes=[
            pltpu.VMEM((HEADS, 2, 4, FRAGMENT, columns), BF16),
            pltpu.VMEM((4, 4, ROWS, D), BF16),
            pltpu.VMEM((4, 4, ROWS, D), BF16),
            pltpu.VMEM((4, 4, KEY_ROWS, D), BF16),
            pltpu.VMEM((8, KEY_ROWS, D), BF16),
            pltpu.VMEM((8, KEY_ROWS, D), BF16),
            pltpu.VMEM((4, KEY_ROWS, D), BF16),
            pltpu.VMEM((D, 3 * LANES), BF16),
            pltpu.VMEM((PATCHES, LANES), BF16),
            pltpu.VMEM((LANES, 2 * PATCHES), BF16),
            pltpu.VMEM((2 * PATCHES, LANES), BF16),
            pltpu.VMEM((16 * KEY_ROWS, 2 * LANES), BF16),
            pltpu.VMEM((8, 16 * KEY_ROWS, 2 * LANES), BF16),
            pltpu.VMEM((4, GROUP, LANES), F32),
            pltpu.VMEM((4, GROUP, LANES), F32),
            pltpu.VMEM((HEADS, HEAD_DIM, BLOCK), BF16),
            pltpu.VMEM((HEADS, HEAD_DIM, BLOCK), BF16),
            pltpu.VMEM((FRAMES, GROUP_ROWS, D), BF16),
            pltpu.VMEM((FRAMES, GROUP_ROWS, D), BF16),
            pltpu.VMEM((FRAMES, GROUP_ROWS, D), BF16),
            pltpu.VMEM((FRAMES, GROUP_ROWS, D), BF16),
            pltpu.VMEM((BLOCK, D), F32),
            pltpu.VMEM((HEADS, HEAD_DIM, BLOCK), F32),
            pltpu.SemaphoreType.DMA((COPIES,)),
            pltpu.SemaphoreType.DMA((COPIES,)),
            pltpu.SemaphoreType.DMA,
        ],
        compiler_params=pltpu.CompilerParams(
            collective_id=1, has_side_effects=True, vmem_limit_bytes=50 * 2**20
        ),
        name="block",
    )(pick, tokens, w, wt, out_w)


def per_device(tokens, key_frame, qkv_spatial, out_spatial, qkv_temporal):
    frame = lax.axis_index("frame")
    key = key_frame[0].astype(jnp.int32)
    y, zl, core = frame // 8, (frame // 2) % 4, frame % 2
    pick = jnp.stack(
        [(key // 8 - y) % 4 * 2 + (key % 2 - core) % 2, (key // 2 % 4 - zl) % 4]
    ).astype(jnp.int32)
    spatial, temporal = block(
        pick, tokens[0], qkv_spatial, qkv_temporal, out_spatial
    )
    return (spatial[None], temporal[None])


def solution(mesh):
    return jax.shard_map(
        per_device,
        mesh=mesh,
        in_specs=(P("frame", "patch", None), P(), P(None, "patch"), P(), P(None, "patch")),
        out_specs=(P("frame", "patch", None), P("frame", "patch", None)),
        check_vma=False,
    )
```

```python
import functools

import jax
import jax.numpy as jnp
from jax import lax
from jax.experimental import pallas as pl
from jax.experimental.pallas import tpu as pltpu
from jax.sharding import PartitionSpec as P

D = 1152
HEADS = 16
HEAD_DIM = 72
PATCHES = 2048
FRAMES = 32
BLOCK = 128
GROUP_ROWS = BLOCK // FRAMES
LANES = 128
CHUNKS = 2
ROWS = BLOCK // CHUNKS
KEY_ROWS = 16
KEY_PAD = 80
FRAGMENT = D // 8
epsilon = 1e-06
LOG2E = 1.4426950408889634
BF16 = jnp.bfloat16
F32 = jnp.float32


def rms_norm(values):
    values = values.astype(F32)
    return values * lax.rsqrt(jnp.mean(values * values, axis=-1, keepdims=True) + epsilon)


def places():
    patch, frame = lax.axis_index("patch"), lax.axis_index("frame")
    return (
        patch,
        frame,
        lax.div(patch, 4),
        lax.rem(patch, 4),
        lax.div(frame, 8),
        lax.rem(lax.div(frame, 2), 4),
        lax.rem(frame, 2),
    )


def turn(at, by):
    return lax.rem(at + by, 4)


class Links:
    def __init__(self, send, recv):
        self.send, self.recv, self.used, self.open = send, recv, 0, []
        self.patch, self.frame, self.x, self.zh, self.y, self.zl, self.core = places()

    def patch_device(self, dx, dz):
        return (self.frame, turn(self.x, dx) * 4 + turn(self.zh, dz))

    def frame_device(self, dy, dz, dc):
        frame = turn(self.y, dy) * 8 + turn(self.zl, dz) * 2 + lax.rem(self.core + dc, 2)
        return (frame, self.patch)

    def frame_at(self, by):
        return (lax.rem(self.frame + by, FRAMES), self.patch)

    def copy(self, src, dst, device):
        made = pltpu.make_async_remote_copy(
            src_ref=src,
            dst_ref=dst,
            send_sem=self.send.at[self.used],
            recv_sem=self.recv.at[self.used],
            device_id=device,
            device_id_type=pl.DeviceIdType.MESH,
        )
        made.start()
        self.used += 1
        self.open.append(made)
        return made

    def finish(self):
        for made in self.open:
            made.wait_send()


def greet(devices, meanwhile):
    barrier = pltpu.get_barrier_semaphore()
    for device in devices:
        pl.semaphore_signal(barrier, inc=1, device_id=device, device_id_type=pl.DeviceIdType.MESH)
    meanwhile()
    pl.semaphore_wait(barrier, len(devices))


class Gather:
    def __init__(self, links, held, rows):
        self.links, self.held, self.rows = links, held, rows
        self.along_x = {}
        self.last = {}

    def halves(self):
        if self.rows % 32:
            return [(pl.ds(0, self.rows), 0)]
        half = self.rows // 2
        return [(pl.ds(0, half), 0), (pl.ds(half, half), 1)]

    def send_x(self, dz):
        links, held = self.links, self.held
        self.along_x[dz] = (
            links.copy(held.at[dz, 0], held.at[dz, 3], links.patch_device(1, 0)),
            links.copy(held.at[dz, 0], held.at[dz, 1], links.patch_device(3, 0)),
        )

    def begin_z(self):
        links, held = self.links, self.held
        self.up = links.copy(held.at[0, 0], held.at[3, 0], links.patch_device(0, 1))
        self.down = links.copy(held.at[0, 0], held.at[1, 0], links.patch_device(0, 3))

    def neighbours(self):
        links, held = self.links, self.held
        self.far = []
        self.up.wait_recv()
        for part, way in self.halves():
            if way == 0:
                self.far.append(
                    links.copy(held.at[3, 0, part], held.at[2, 0, part], links.patch_device(0, 1))
                )
        self.send_x(3)
        self.down.wait_recv()
        for part, way in self.halves():
            if way == 1:
                self.far.append(
                    links.copy(held.at[1, 0, part], held.at[2, 0, part], links.patch_device(0, 3))
                )
        self.send_x(1)

    def opposite(self):
        for made in self.far:
            made.wait_recv()
        self.send_x(2)

    def forward_x(self, dz):
        links, held = self.links, self.held
        up, down = self.along_x[dz]
        self.last[dz] = []
        up.wait_recv()
        for part, way in self.halves():
            if way == 0:
                self.last[dz].append(
                    links.copy(held.at[dz, 3, part], held.at[dz, 2, part], links.patch_device(1, 0))
                )
        down.wait_recv()
        for part, way in self.halves():
            if way == 1:
                self.last[dz].append(
                    links.copy(held.at[dz, 1, part], held.at[dz, 2, part], links.patch_device(3, 0))
                )

    def done_x(self, dz):
        for made in self.last[dz]:
            made.wait_recv()


def with_ones(values):
    lane = lax.broadcasted_iota(jnp.int32, values.shape, 1)
    return jnp.where(lane == HEAD_DIM, jnp.ones_like(values), values)


GATHER_COPIES = 20
COPIES = (CHUNKS + 1) * GATHER_COPIES + 7 + 3 + 7 + 3 + 6 + 6 + 8 + 15 + 62
SPLIT = 64
GROUP = 512


HEAD_STEP = 4


def scatter(links, values, out, landing):
    for f in range(FRAMES):
        out[f] = values[f * GROUP_ROWS : (f + 1) * GROUP_ROWS].astype(BF16)
    links.slots = [
        links.copy(
            out.at[lax.rem(links.frame + k, FRAMES)], landing.at[links.frame], links.frame_at(k)
        )
        for k in range(1, FRAMES)
    ]
    landing[links.frame] = out[links.frame]


def collect(links, landing, flat):
    for made in links.slots:
        made.wait_recv()
    for f in range(FRAMES):
        flat[f * GROUP_ROWS : (f + 1) * GROUP_ROWS, :] = landing[f].astype(F32)


def mix(rows, wt, turned, first):
    row = lax.broadcasted_iota(jnp.int32, (BLOCK, BLOCK), 0)
    column = lax.broadcasted_iota(jnp.int32, (BLOCK, BLOCK), 1)
    same = lax.rem(row, GROUP_ROWS) == lax.rem(column, GROUP_ROWS)
    heads = [first + i for i in range(HEAD_STEP)]
    qkv = [
        jnp.dot(
            rows, wt[h].reshape(D, 3 * HEAD_DIM), preferred_element_type=F32
        ).astype(BF16)
        for h in heads
    ]
    scores = [
        lax.dot_general(
            one[:, :HEAD_DIM],
            one[:, HEAD_DIM : 2 * HEAD_DIM],
            (((1,), (1,)), ((), ())),
            preferred_element_type=F32,
        )
        * (HEAD_DIM**-0.5)
        for one in qkv
    ]
    scores = [jnp.where(same, one, -jnp.inf) for one in scores]
    largest = [jnp.max(one, axis=-1, keepdims=True) for one in scores]
    exponent = [jnp.exp(one - top) for one, top in zip(scores, largest)]
    sums = [jnp.sum(one, axis=-1, keepdims=True) for one in exponent]
    weights = [(one / total).astype(BF16) for one, total in zip(exponent, sums)]
    outs = [
        jnp.dot(one, values, preferred_element_type=F32) for one, values in zip(weights, qkv)
    ]
    for h, out in zip(heads, outs):
        turned[h] = out.T[2 * HEAD_DIM :, :]


def block_kernel(
    pick_ref,
    tokens_ref,
    w_ref,
    wt_ref,
    out_w_ref,
    spatial_ref,
    temporal_ref,
    wt,
    held0,
    held1,
    kheld,
    slices,
    first,
    second,
    w,
    q_s,
    kt,
    v_s,
    kv_out,
    kv_in,
    total_s,
    largest_s,
    out_s,
    heads,
    rows_out,
    rows_in,
    mixed_out,
    mixed_in,
    flat,
    head_rows,
    send,
    recv,
    local_sem,
):
    links = Links(send, recv)
    x, y, core = links.x, links.y, links.core
    others = [(dy, dc) for dy in range(4) for dc in range(2) if (dy, dc) != (0, 0)]
    turns = [(dz, dx) for dz in (0, 3, 1, 2) for dx in range(4)]
    held = (held0, held1)

    def prepare():
        normed = rms_norm(tokens_ref[...]).astype(BF16)
        for g in range(8):
            slices[g] = normed[g * KEY_ROWS : (g + 1) * KEY_ROWS]
        for c in range(CHUNKS):
            held[c][0, 0] = normed[c * ROWS : (c + 1) * ROWS]

    greet(
        [links.patch_device(dx, dz) for dz, dx in turns if (dz, dx) != (0, 0)]
        + [links.frame_at(k) for k in range(1, FRAMES)],
        prepare,
    )
    picks = []
    for dy, dc in others:
        there = turn(y, dy) * 2 + lax.rem(core + dc, 2)
        slot = (4 - dy) % 4 * 2 + dc
        picks.append(
            links.copy(slices.at[there], first.at[slot], links.frame_device(dy, 0, dc))
        )
    gathers = [Gather(links, held[c], ROWS) for c in range(CHUNKS)]
    gathers[0].begin_z()
    for one in gathers:
        one.send_x(0)
    mine = wt_ref.at[pl.ds(pl.multiple_of((core * 4 + y) * FRAGMENT, 16), FRAGMENT)]
    place = wt.at[links.patch, core, y]
    own = pltpu.make_async_copy(mine, place, local_sem)
    own.start()
    first[0] = slices[y * 2 + core]
    for made in picks:
        made.wait_recv()
    second[0] = first[pick_ref[0]]
    picks = [
        links.copy(second.at[0], second.at[4 - dz], links.frame_device(0, dz, 0))
        for dz in (1, 2, 3)
    ]
    gathers[1].begin_z()
    w[...] = jnp.zeros_like(w)
    kt[KEY_PAD:, PATCHES:] = jnp.zeros((LANES - KEY_PAD, PATCHES), BF16)
    for i in range(3):
        w[:, i * LANES : i * LANES + HEAD_DIM] = w_ref[:, i * HEAD_DIM : (i + 1) * HEAD_DIM]
    for one in gathers:
        one.forward_x(0)
    gathers[0].neighbours()
    for made in picks:
        made.wait_recv()
    kheld[0, 0] = second[pick_ref[1]]
    keys = Gather(links, kheld, KEY_ROWS)
    keys.begin_z()
    keys.send_x(0)
    gathers[1].neighbours()
    wt_up = links.copy(mine, place, links.patch_device(0, 1))
    wt_down = links.copy(mine, place, links.patch_device(0, 3))
    keys.neighbours()
    keys.forward_x(0)

    def finish(dz):
        for c in range(CHUNKS):
            gathers[c].done_x(dz)
            out = jnp.dot(
                held[c][dz].reshape(4 * ROWS, D), w[...], preferred_element_type=F32
            )
            q = (out[:, :LANES] * (HEAD_DIM**-0.5 * LOG2E)).astype(BF16)
            for dx in range(4):
                at = (dz * 4 + dx) * BLOCK + c * ROWS
                q_s[at : at + ROWS, :] = q[dx * ROWS : (dx + 1) * ROWS]
            at = (dz * CHUNKS + c) * 4 * ROWS
            kt[:, at : at + 4 * ROWS] = out[:, LANES : 2 * LANES].T.astype(BF16)
            v_s[at : at + 4 * ROWS, :] = with_ones(out[:, 2 * LANES :]).astype(BF16)

    finish(0)
    for dz in (3, 1):
        for one in (gathers[0], gathers[1]):
            one.forward_x(dz)
    for one in (gathers[0], gathers[1]):
        one.opposite()
    for dz in (3, 1):
        keys.forward_x(dz)
    keys.opposite()
    finish(3)
    finish(1)
    for one in (gathers[0], gathers[1], keys):
        one.forward_x(2)
    for dz in range(4):
        keys.done_x(dz)
    out = jnp.dot(
        kheld[...].reshape(16 * KEY_ROWS, D), w[:, LANES:], preferred_element_type=F32
    )
    kv_out[:KEY_PAD, :] = out[:, :LANES].T[:KEY_PAD].astype(BF16)
    values = with_ones(out[:, LANES:]).astype(BF16)
    kv_out[KEY_PAD:, :LANES] = values[:LANES]
    kv_out[KEY_PAD:, LANES:] = values[LANES:]
    twin = links.frame_device(0, 0, 1)
    kv_y = [
        (links.copy(kv_out, kv_in.at[(4 - d) * 2], links.frame_device(d, 0, 0)), (4 - d) * 2)
        for d in (1, 3, 2)
    ]
    kv_twin = [links.copy(kv_out, kv_in.at[1], twin)]
    wt_up.wait_recv()
    below = wt.at[x * 4 + turn(links.zh, 3), core, y]
    wt_far = links.copy(below, below, links.patch_device(0, 1))
    finish(2)
    own.wait()
    wt_down.wait_recv()
    wt_far.wait_recv()
    group = pl.ds(x * 4, 4)
    upper, lower = pl.ds(0, SPLIT), pl.ds(SPLIT, FRAGMENT - SPLIT)
    by_y, by_x = wt.at[group, core, y, upper], wt.at[group, core, y, lower]
    steps = []
    for d in (1, 3, 2):
        steps.append(links.copy(by_y, by_y, links.frame_device(d, 0, 0)))
        steps.append(links.copy(by_x, by_x, links.patch_device(d, 0)))

    def along_x(dx, rows=upper, half=slice(0, 4)):
        return wt.at[pl.ds(turn(x, dx) * 4, 4), core, pl.ds(half.start, half.stop - half.start), rows]

    def along_y(dy, half=slice(0, 16)):
        return wt.at[pl.ds(half.start, half.stop - half.start), core, turn(y, dy), lower]

    def pass_on(piece, device):
        return links.copy(piece, piece, device)

    def scores_of(g, keys):
        q = q_s[g * GROUP : (g + 1) * GROUP, :]
        scores = jnp.dot(q, kt[:, keys], preferred_element_type=F32)
        return scores, jnp.max(scores, axis=-1, keepdims=True)

    for g in range(4):
        scores, largest = scores_of(g, slice(0, PATCHES))
        weights = jnp.exp2(scores - largest).astype(BF16)
        total_s[g] = jnp.dot(weights, v_s[:PATCHES, :], preferred_element_type=F32)
        largest_s[g] = jnp.broadcast_to(largest, (GROUP, LANES))
        if g == 0:
            for made, slot in kv_y:
                made.wait_recv()
                kv_twin.append(links.copy(kv_in.at[slot], kv_in.at[slot + 1], twin))
    for made in steps:
        made.wait_recv()
    x_up = pass_on(along_x(0), links.patch_device(1, 0))
    x_down = pass_on(along_x(0), links.patch_device(3, 0))
    y_up = pass_on(along_y(0), links.frame_device(1, 0, 0))
    y_down = pass_on(along_y(0), links.frame_device(3, 0, 0))
    cross_x, cross_y = [pass_on(along_x(0), twin)], [pass_on(along_y(0), twin)]
    kv_in[0] = kv_out[...]
    for made in kv_twin:
        made.wait_recv()
    for g in range(8):
        at = PATCHES + g * 16 * KEY_ROWS
        kt[:KEY_PAD, at : at + 16 * KEY_ROWS] = kv_in[g, :KEY_PAD, :]
        v_s[at : at + LANES, :] = kv_in[g, KEY_PAD:, :LANES]
        v_s[at + LANES : at + 2 * LANES, :] = kv_in[g, KEY_PAD:, LANES:]
    sent = []
    for g in (2, 3, 1, 0):
        scores, new = scores_of(g, slice(PATCHES, 2 * PATCHES))
        largest = largest_s[g][:, :1]
        new = jnp.maximum(largest, new)
        weights = jnp.exp2(scores - new).astype(BF16)
        total = total_s[g] * jnp.exp2(largest - new) + jnp.dot(
            weights, v_s[PATCHES:, :], preferred_element_type=F32
        )
        turned = (total / total[:, HEAD_DIM : HEAD_DIM + 1]).T
        for dx in (2, 1, 3, 0):
            block = turned[:HEAD_DIM, dx * BLOCK : (dx + 1) * BLOCK].astype(BF16)
            if (g, dx) == (0, 0):
                heads[links.patch] = block
            else:
                out_s[g * 4 + dx] = block
                sent.append(
                    links.copy(
                        out_s.at[g * 4 + dx], heads.at[links.patch], links.patch_device(dx, g)
                    )
                )
    for made in sent:
        made.wait_recv()
    rows = heads[...].reshape(D, BLOCK).T
    spatial = jnp.dot(rows, out_w_ref[...], preferred_element_type=F32).astype(BF16)
    spatial_ref[...] = spatial
    scatter(links, rms_norm(spatial), rows_out, rows_in)
    y_up.wait_recv()
    far_y = [pass_on(along_y(3, slice(0, 8)), links.frame_device(1, 0, 0))]
    cross_y.append(pass_on(along_y(3), twin))
    x_up.wait_recv()
    far_x = [pass_on(along_x(3, half=slice(0, 2)), links.patch_device(1, 0))]
    cross_x.append(pass_on(along_x(3), twin))
    y_down.wait_recv()
    far_y.append(pass_on(along_y(1, slice(8, 16)), links.frame_device(3, 0, 0)))
    cross_y.append(pass_on(along_y(1), twin))
    x_down.wait_recv()
    far_x.append(pass_on(along_x(1, half=slice(2, 4)), links.patch_device(3, 0)))
    cross_x.append(pass_on(along_x(1), twin))
    collect(links, rows_in, flat)
    rows = flat[...].astype(BF16)
    for made in far_y:
        made.wait_recv()
    cross_y.append(pass_on(along_y(2), twin))
    for made in cross_y:
        made.wait_recv()
    for i, dx in enumerate((0, 3, 1, 2)):
        if i == 1:
            for made in far_x:
                made.wait_recv()
            cross_x.append(pass_on(along_x(2), twin))
        cross_x[i].wait_recv()
        mix(rows, wt, head_rows, turn(x, dx) * 4)
    scatter(links, head_rows[...].reshape(D, BLOCK).T, mixed_out, mixed_in)
    collect(links, mixed_in, flat)
    temporal_ref[...] = flat[...].astype(BF16)
    links.finish()


def block(pick, tokens, w, wt, out_w):
    vmem = pl.BlockSpec(memory_space=pltpu.VMEM)
    anywhere = pl.BlockSpec(memory_space=pl.ANY)
    columns = wt.shape[1]
    return pl.pallas_call(
        block_kernel,
        out_shape=[
            jax.ShapeDtypeStruct((BLOCK, D), BF16),
            jax.ShapeDtypeStruct((BLOCK, D), BF16),
        ],
        in_specs=[pl.BlockSpec(memory_space=pltpu.SMEM), vmem, vmem, anywhere, vmem],
        out_specs=[vmem, vmem],
        scratch_shapes=[
            pltpu.VMEM((HEADS, 2, 4, FRAGMENT, columns), BF16),
            pltpu.VMEM((4, 4, ROWS, D), BF16),
            pltpu.VMEM((4, 4, ROWS, D), BF16),
            pltpu.VMEM((4, 4, KEY_ROWS, D), BF16),
            pltpu.VMEM((8, KEY_ROWS, D), BF16),
            pltpu.VMEM((8, KEY_ROWS, D), BF16),
            pltpu.VMEM((4, KEY_ROWS, D), BF16),
            pltpu.VMEM((D, 3 * LANES), BF16),
            pltpu.VMEM((PATCHES, LANES), BF16),
            pltpu.VMEM((LANES, 2 * PATCHES), BF16),
            pltpu.VMEM((2 * PATCHES, LANES), BF16),
            pltpu.VMEM((KEY_PAD + LANES, 2 * LANES), BF16),
            pltpu.VMEM((8, KEY_PAD + LANES, 2 * LANES), BF16),
            pltpu.VMEM((4, GROUP, LANES), F32),
            pltpu.VMEM((4, GROUP, LANES), F32),
            pltpu.VMEM((HEADS, HEAD_DIM, BLOCK), BF16),
            pltpu.VMEM((HEADS, HEAD_DIM, BLOCK), BF16),
            pltpu.VMEM((FRAMES, GROUP_ROWS, D), BF16),
            pltpu.VMEM((FRAMES, GROUP_ROWS, D), BF16),
            pltpu.VMEM((FRAMES, GROUP_ROWS, D), BF16),
            pltpu.VMEM((FRAMES, GROUP_ROWS, D), BF16),
            pltpu.VMEM((BLOCK, D), F32),
            pltpu.VMEM((HEADS, HEAD_DIM, BLOCK), F32),
            pltpu.SemaphoreType.DMA((COPIES,)),
            pltpu.SemaphoreType.DMA((COPIES,)),
            pltpu.SemaphoreType.DMA,
        ],
        compiler_params=pltpu.CompilerParams(
            collective_id=1, has_side_effects=True, vmem_limit_bytes=50 * 2**20
        ),
        name="block",
    )(pick, tokens, w, wt, out_w)


def per_device(tokens, key_frame, qkv_spatial, out_spatial, qkv_temporal):
    frame = lax.axis_index("frame")
    key = key_frame[0].astype(jnp.int32)
    y, zl, core = frame // 8, (frame // 2) % 4, frame % 2
    pick = jnp.stack(
        [(key // 8 - y) % 4 * 2 + (key % 2 - core) % 2, (key // 2 % 4 - zl) % 4]
    ).astype(jnp.int32)
    spatial, temporal = block(
        pick, tokens[0], qkv_spatial, qkv_temporal, out_spatial
    )
    return (spatial[None], temporal[None])


def solution(mesh):
    return jax.shard_map(
        per_device,
        mesh=mesh,
        in_specs=(P("frame", "patch", None), P(), P(None, "patch"), P(), P(None, "patch")),
        out_specs=(P("frame", "patch", None), P("frame", "patch", None)),
        check_vma=False,
    )
```

```python
import functools

import jax
import jax.numpy as jnp
from jax import lax
from jax.experimental import pallas as pl
from jax.experimental.pallas import tpu as pltpu
from jax.sharding import PartitionSpec as P

D = 1152
HEADS = 16
HEAD_DIM = 72
PATCHES = 2048
FRAMES = 32
BLOCK = 128
GROUP_ROWS = BLOCK // FRAMES
LANES = 128
CHUNKS = 2
ROWS = BLOCK // CHUNKS
KEY_ROWS = 16
KEY_PAD = 80
FRAGMENT = D // 8
epsilon = 1e-06
LOG2E = 1.4426950408889634
BF16 = jnp.bfloat16
F32 = jnp.float32


def rms_norm(values):
    values = values.astype(F32)
    return values * lax.rsqrt(jnp.mean(values * values, axis=-1, keepdims=True) + epsilon)


def places():
    patch, frame = lax.axis_index("patch"), lax.axis_index("frame")
    return (
        patch,
        frame,
        lax.div(patch, 4),
        lax.rem(patch, 4),
        lax.div(frame, 8),
        lax.rem(lax.div(frame, 2), 4),
        lax.rem(frame, 2),
    )


def turn(at, by):
    return lax.rem(at + by, 4)


class Links:
    def __init__(self, send, recv):
        self.send, self.recv, self.used, self.open = send, recv, 0, []
        self.patch, self.frame, self.x, self.zh, self.y, self.zl, self.core = places()

    def patch_device(self, dx, dz):
        return (self.frame, turn(self.x, dx) * 4 + turn(self.zh, dz))

    def frame_device(self, dy, dz, dc):
        frame = turn(self.y, dy) * 8 + turn(self.zl, dz) * 2 + lax.rem(self.core + dc, 2)
        return (frame, self.patch)

    def frame_at(self, by):
        return (lax.rem(self.frame + by, FRAMES), self.patch)

    def copy(self, src, dst, device):
        made = pltpu.make_async_remote_copy(
            src_ref=src,
            dst_ref=dst,
            send_sem=self.send.at[self.used],
            recv_sem=self.recv.at[self.used],
            device_id=device,
            device_id_type=pl.DeviceIdType.MESH,
        )
        made.start()
        self.used += 1
        self.open.append(made)
        return made

    def finish(self):
        for made in self.open:
            made.wait_send()


def greet(devices, meanwhile):
    barrier = pltpu.get_barrier_semaphore()
    for device in devices:
        pl.semaphore_signal(barrier, inc=1, device_id=device, device_id_type=pl.DeviceIdType.MESH)
    meanwhile()
    pl.semaphore_wait(barrier, len(devices))


class Gather:
    def __init__(self, links, held, rows):
        self.links, self.held, self.rows = links, held, rows
        self.along_x = {}
        self.last = {}

    def halves(self):
        if self.rows % 32:
            return [(pl.ds(0, self.rows), 0)]
        half = self.rows // 2
        return [(pl.ds(0, half), 0), (pl.ds(half, half), 1)]

    def send_x(self, dz):
        links, held = self.links, self.held
        self.along_x[dz] = (
            links.copy(held.at[dz, 0], held.at[dz, 3], links.patch_device(1, 0)),
            links.copy(held.at[dz, 0], held.at[dz, 1], links.patch_device(3, 0)),
        )

    def begin_z(self):
        links, held = self.links, self.held
        self.up = links.copy(held.at[0, 0], held.at[3, 0], links.patch_device(0, 1))
        self.down = links.copy(held.at[0, 0], held.at[1, 0], links.patch_device(0, 3))

    def neighbours(self):
        links, held = self.links, self.held
        self.far = []
        self.up.wait_recv()
        for part, way in self.halves():
            if way == 0:
                self.far.append(
                    links.copy(held.at[3, 0, part], held.at[2, 0, part], links.patch_device(0, 1))
                )
        self.send_x(3)
        self.down.wait_recv()
        for part, way in self.halves():
            if way == 1:
                self.far.append(
                    links.copy(held.at[1, 0, part], held.at[2, 0, part], links.patch_device(0, 3))
                )
        self.send_x(1)

    def opposite(self):
        for made in self.far:
            made.wait_recv()
        self.send_x(2)

    def forward_x(self, dz):
        links, held = self.links, self.held
        up, down = self.along_x[dz]
        self.last[dz] = []
        up.wait_recv()
        for part, way in self.halves():
            if way == 0:
                self.last[dz].append(
                    links.copy(held.at[dz, 3, part], held.at[dz, 2, part], links.patch_device(1, 0))
                )
        down.wait_recv()
        for part, way in self.halves():
            if way == 1:
                self.last[dz].append(
                    links.copy(held.at[dz, 1, part], held.at[dz, 2, part], links.patch_device(3, 0))
                )

    def done_x(self, dz):
        for made in self.last[dz]:
            made.wait_recv()


def with_ones(values):
    lane = lax.broadcasted_iota(jnp.int32, values.shape, 1)
    return jnp.where(lane == HEAD_DIM, jnp.ones_like(values), values)


GATHER_COPIES = 20
COPIES = (CHUNKS + 1) * GATHER_COPIES + 7 + 3 + 7 + 3 + 6 + 6 + 8 + 15 + 62
SPLIT = 64
GROUP = 512


HEAD_STEP = 4


def scatter(links, values, out, landing):
    for f in range(FRAMES):
        out[f] = values[f * GROUP_ROWS : (f + 1) * GROUP_ROWS].astype(BF16)
    links.slots = [
        links.copy(
            out.at[lax.rem(links.frame + k, FRAMES)], landing.at[links.frame], links.frame_at(k)
        )
        for k in range(1, FRAMES)
    ]
    landing[links.frame] = out[links.frame]


def collect(links, landing, flat):
    for made in links.slots:
        made.wait_recv()
    for f in range(FRAMES):
        flat[f * GROUP_ROWS : (f + 1) * GROUP_ROWS, :] = landing[f].astype(F32)


def mix(rows, wt, turned, first):
    row = lax.broadcasted_iota(jnp.int32, (BLOCK, BLOCK), 0)
    column = lax.broadcasted_iota(jnp.int32, (BLOCK, BLOCK), 1)
    same = lax.rem(row, GROUP_ROWS) == lax.rem(column, GROUP_ROWS)
    heads = range(first, first + HEAD_STEP)
    qkv = [
        jnp.dot(
            rows, wt[h].reshape(D, 3 * HEAD_DIM), preferred_element_type=F32
        ).astype(BF16)
        for h in heads
    ]
    scores = [
        lax.dot_general(
            one[:, :HEAD_DIM],
            one[:, HEAD_DIM : 2 * HEAD_DIM],
            (((1,), (1,)), ((), ())),
            preferred_element_type=F32,
        )
        * (HEAD_DIM**-0.5)
        for one in qkv
    ]
    scores = [jnp.where(same, one, -jnp.inf) for one in scores]
    largest = [jnp.max(one, axis=-1, keepdims=True) for one in scores]
    exponent = [jnp.exp(one - top) for one, top in zip(scores, largest)]
    sums = [jnp.sum(one, axis=-1, keepdims=True) for one in exponent]
    weights = [(one / total).astype(BF16) for one, total in zip(exponent, sums)]
    outs = [
        jnp.dot(one, values, preferred_element_type=F32) for one, values in zip(weights, qkv)
    ]
    for h, out in zip(heads, outs):
        turned[h] = out.T[2 * HEAD_DIM :, :]


def block_kernel(
    pick_ref,
    tokens_ref,
    w_ref,
    wt_ref,
    out_w_ref,
    spatial_ref,
    temporal_ref,
    wt,
    held0,
    held1,
    kheld,
    slices,
    first,
    second,
    w,
    q_s,
    kt,
    v_s,
    kv_out,
    kv_in,
    total_s,
    largest_s,
    out_s,
    heads,
    rows_out,
    rows_in,
    mixed_out,
    mixed_in,
    flat,
    head_rows,
    send,
    recv,
    local_sem,
):
    links = Links(send, recv)
    x, y, core = links.x, links.y, links.core
    others = [(dy, dc) for dy in range(4) for dc in range(2) if (dy, dc) != (0, 0)]
    turns = [(dz, dx) for dz in (0, 3, 1, 2) for dx in range(4)]
    held = (held0, held1)

    def prepare():
        normed = rms_norm(tokens_ref[...]).astype(BF16)
        for g in range(8):
            slices[g] = normed[g * KEY_ROWS : (g + 1) * KEY_ROWS]
        for c in range(CHUNKS):
            held[c][0, 0] = normed[c * ROWS : (c + 1) * ROWS]

    greet(
        [links.patch_device(dx, dz) for dz, dx in turns if (dz, dx) != (0, 0)]
        + [links.frame_at(k) for k in range(1, FRAMES)],
        prepare,
    )
    picks = []
    for dy, dc in others:
        there = turn(y, dy) * 2 + lax.rem(core + dc, 2)
        slot = (4 - dy) % 4 * 2 + dc
        picks.append(
            links.copy(slices.at[there], first.at[slot], links.frame_device(dy, 0, dc))
        )
    gathers = [Gather(links, held[c], ROWS) for c in range(CHUNKS)]
    gathers[0].begin_z()
    for one in gathers:
        one.send_x(0)
    mine = wt_ref.at[pl.ds(pl.multiple_of((core * 4 + y) * FRAGMENT, 16), FRAGMENT)]
    place = wt.at[links.patch, core, y]
    own = pltpu.make_async_copy(mine, place, local_sem)
    own.start()
    first[0] = slices[y * 2 + core]
    for made in picks:
        made.wait_recv()
    second[0] = first[pick_ref[0]]
    picks = [
        links.copy(second.at[0], second.at[4 - dz], links.frame_device(0, dz, 0))
        for dz in (1, 2, 3)
    ]
    gathers[1].begin_z()
    w[...] = jnp.zeros_like(w)
    kt[KEY_PAD:, PATCHES:] = jnp.zeros((LANES - KEY_PAD, PATCHES), BF16)
    for i in range(3):
        w[:, i * LANES : i * LANES + HEAD_DIM] = w_ref[:, i * HEAD_DIM : (i + 1) * HEAD_DIM]
    for one in gathers:
        one.forward_x(0)
    gathers[0].neighbours()
    for made in picks:
        made.wait_recv()
    kheld[0, 0] = second[pick_ref[1]]
    keys = Gather(links, kheld, KEY_ROWS)
    keys.begin_z()
    keys.send_x(0)
    gathers[1].neighbours()
    wt_up = links.copy(mine, place, links.patch_device(0, 1))
    wt_down = links.copy(mine, place, links.patch_device(0, 3))
    keys.neighbours()
    keys.forward_x(0)

    def finish(dz):
        for c in range(CHUNKS):
            gathers[c].done_x(dz)
            out = jnp.dot(
                held[c][dz].reshape(4 * ROWS, D), w[...], preferred_element_type=F32
            )
            q = (out[:, :LANES] * (HEAD_DIM**-0.5 * LOG2E)).astype(BF16)
            for dx in range(4):
                at = (dz * 4 + dx) * BLOCK + c * ROWS
                q_s[at : at + ROWS, :] = q[dx * ROWS : (dx + 1) * ROWS]
            at = (dz * CHUNKS + c) * 4 * ROWS
            kt[:, at : at + 4 * ROWS] = out[:, LANES : 2 * LANES].T.astype(BF16)
            v_s[at : at + 4 * ROWS, :] = with_ones(out[:, 2 * LANES :]).astype(BF16)

    finish(0)
    for dz in (3, 1):
        for one in (gathers[0], gathers[1]):
            one.forward_x(dz)
    for one in (gathers[0], gathers[1]):
        one.opposite()
    for dz in (3, 1):
        keys.forward_x(dz)
    keys.opposite()
    finish(3)
    finish(1)
    for one in (gathers[0], gathers[1], keys):
        one.forward_x(2)
    wt_up.wait_recv()
    below = wt.at[x * 4 + turn(links.zh, 3), core, y]
    wt_far = links.copy(below, below, links.patch_device(0, 1))
    for dz in range(4):
        keys.done_x(dz)
    out = jnp.dot(
        kheld[...].reshape(16 * KEY_ROWS, D), w[:, LANES:], preferred_element_type=F32
    )
    kv_out[:KEY_PAD, :] = out[:, :LANES].T[:KEY_PAD].astype(BF16)
    values = with_ones(out[:, LANES:]).astype(BF16)
    kv_out[KEY_PAD:, :LANES] = values[:LANES]
    kv_out[KEY_PAD:, LANES:] = values[LANES:]
    twin = links.frame_device(0, 0, 1)
    kv_y = [
        (links.copy(kv_out, kv_in.at[(4 - d) * 2], links.frame_device(d, 0, 0)), (4 - d) * 2)
        for d in (1, 3, 2)
    ]
    kv_twin = [links.copy(kv_out, kv_in.at[1], twin)]
    finish(2)
    own.wait()
    wt_down.wait_recv()
    wt_far.wait_recv()
    group = pl.ds(x * 4, 4)
    upper, lower = pl.ds(0, SPLIT), pl.ds(SPLIT, FRAGMENT - SPLIT)
    by_y, by_x = wt.at[group, core, y, upper], wt.at[group, core, y, lower]
    steps = []
    for d in (1, 3, 2):
        steps.append(links.copy(by_y, by_y, links.frame_device(d, 0, 0)))
        steps.append(links.copy(by_x, by_x, links.patch_device(d, 0)))

    def along_x(dx, rows=upper, half=slice(0, 4)):
        return wt.at[pl.ds(turn(x, dx) * 4, 4), core, pl.ds(half.start, half.stop - half.start), rows]

    def along_y(dy, half=slice(0, 16)):
        return wt.at[pl.ds(half.start, half.stop - half.start), core, turn(y, dy), lower]

    def pass_on(piece, device):
        return links.copy(piece, piece, device)

    def scores_of(g, keys):
        q = q_s[g * GROUP : (g + 1) * GROUP, :]
        scores = jnp.dot(q, kt[:, keys], preferred_element_type=F32)
        return scores, jnp.max(scores, axis=-1, keepdims=True)

    for g in range(4):
        scores, largest = scores_of(g, slice(0, PATCHES))
        weights = jnp.exp2(scores - largest).astype(BF16)
        total_s[g] = jnp.dot(weights, v_s[:PATCHES, :], preferred_element_type=F32)
        largest_s[g] = jnp.broadcast_to(largest, (GROUP, LANES))
        if g == 0:
            for made, slot in kv_y:
                made.wait_recv()
                kv_twin.append(links.copy(kv_in.at[slot], kv_in.at[slot + 1], twin))
    for made in steps:
        made.wait_recv()
    x_up = pass_on(along_x(0), links.patch_device(1, 0))
    x_down = pass_on(along_x(0), links.patch_device(3, 0))
    y_up = pass_on(along_y(0), links.frame_device(1, 0, 0))
    y_down = pass_on(along_y(0), links.frame_device(3, 0, 0))
    cross = [pass_on(along_x(0), twin), pass_on(along_y(0), twin)]
    kv_in[0] = kv_out[...]
    for made in kv_twin:
        made.wait_recv()
    for g in range(8):
        at = PATCHES + g * 16 * KEY_ROWS
        kt[:KEY_PAD, at : at + 16 * KEY_ROWS] = kv_in[g, :KEY_PAD, :]
        v_s[at : at + LANES, :] = kv_in[g, KEY_PAD:, :LANES]
        v_s[at + LANES : at + 2 * LANES, :] = kv_in[g, KEY_PAD:, LANES:]
    sent = []
    for g in (2, 3, 1, 0):
        scores, new = scores_of(g, slice(PATCHES, 2 * PATCHES))
        largest = largest_s[g][:, :1]
        new = jnp.maximum(largest, new)
        weights = jnp.exp2(scores - new).astype(BF16)
        total = total_s[g] * jnp.exp2(largest - new) + jnp.dot(
            weights, v_s[PATCHES:, :], preferred_element_type=F32
        )
        turned = (total / total[:, HEAD_DIM : HEAD_DIM + 1]).T
        for dx in (2, 1, 3, 0):
            block = turned[:HEAD_DIM, dx * BLOCK : (dx + 1) * BLOCK].astype(BF16)
            if (g, dx) == (0, 0):
                heads[links.patch] = block
            else:
                out_s[g * 4 + dx] = block
                sent.append(
                    links.copy(
                        out_s.at[g * 4 + dx], heads.at[links.patch], links.patch_device(dx, g)
                    )
                )
    for made in sent:
        made.wait_recv()
    rows = heads[...].reshape(D, BLOCK).T
    spatial = jnp.dot(rows, out_w_ref[...], preferred_element_type=F32).astype(BF16)
    spatial_ref[...] = spatial
    scatter(links, rms_norm(spatial), rows_out, rows_in)
    x_up.wait_recv()
    far = [pass_on(along_x(3, half=slice(0, 2)), links.patch_device(1, 0))]
    cross.append(pass_on(along_x(3), twin))
    y_up.wait_recv()
    far.append(pass_on(along_y(3, slice(0, 8)), links.frame_device(1, 0, 0)))
    cross.append(pass_on(along_y(3), twin))
    x_down.wait_recv()
    far.append(pass_on(along_x(1, half=slice(2, 4)), links.patch_device(3, 0)))
    cross.append(pass_on(along_x(1), twin))
    y_down.wait_recv()
    far.append(pass_on(along_y(1, slice(8, 16)), links.frame_device(3, 0, 0)))
    cross.append(pass_on(along_y(1), twin))
    for made in far:
        made.wait_recv()
    cross.append(pass_on(along_x(2), twin))
    cross.append(pass_on(along_y(2), twin))
    collect(links, rows_in, flat)
    rows = flat[...].astype(BF16)
    for made in cross:
        made.wait_recv()
    for h in range(0, HEADS, HEAD_STEP):
        mix(rows, wt, head_rows, h)
    scatter(links, head_rows[...].reshape(D, BLOCK).T, mixed_out, mixed_in)
    collect(links, mixed_in, flat)
    temporal_ref[...] = flat[...].astype(BF16)
    links.finish()


def block(pick, tokens, w, wt, out_w):
    vmem = pl.BlockSpec(memory_space=pltpu.VMEM)
    anywhere = pl.BlockSpec(memory_space=pl.ANY)
    columns = wt.shape[1]
    return pl.pallas_call(
        block_kernel,
        out_shape=[
            jax.ShapeDtypeStruct((BLOCK, D), BF16),
            jax.ShapeDtypeStruct((BLOCK, D), BF16),
        ],
        in_specs=[pl.BlockSpec(memory_space=pltpu.SMEM), vmem, vmem, anywhere, vmem],
        out_specs=[vmem, vmem],
        scratch_shapes=[
            pltpu.VMEM((HEADS, 2, 4, FRAGMENT, columns), BF16),
            pltpu.VMEM((4, 4, ROWS, D), BF16),
            pltpu.VMEM((4, 4, ROWS, D), BF16),
            pltpu.VMEM((4, 4, KEY_ROWS, D), BF16),
            pltpu.VMEM((8, KEY_ROWS, D), BF16),
            pltpu.VMEM((8, KEY_ROWS, D), BF16),
            pltpu.VMEM((4, KEY_ROWS, D), BF16),
            pltpu.VMEM((D, 3 * LANES), BF16),
            pltpu.VMEM((PATCHES, LANES), BF16),
            pltpu.VMEM((LANES, 2 * PATCHES), BF16),
            pltpu.VMEM((2 * PATCHES, LANES), BF16),
            pltpu.VMEM((KEY_PAD + LANES, 2 * LANES), BF16),
            pltpu.VMEM((8, KEY_PAD + LANES, 2 * LANES), BF16),
            pltpu.VMEM((4, GROUP, LANES), F32),
            pltpu.VMEM((4, GROUP, LANES), F32),
            pltpu.VMEM((HEADS, HEAD_DIM, BLOCK), BF16),
            pltpu.VMEM((HEADS, HEAD_DIM, BLOCK), BF16),
            pltpu.VMEM((FRAMES, GROUP_ROWS, D), BF16),
            pltpu.VMEM((FRAMES, GROUP_ROWS, D), BF16),
            pltpu.VMEM((FRAMES, GROUP_ROWS, D), BF16),
            pltpu.VMEM((FRAMES, GROUP_ROWS, D), BF16),
            pltpu.VMEM((BLOCK, D), F32),
            pltpu.VMEM((HEADS, HEAD_DIM, BLOCK), F32),
            pltpu.SemaphoreType.DMA((COPIES,)),
            pltpu.SemaphoreType.DMA((COPIES,)),
            pltpu.SemaphoreType.DMA,
        ],
        compiler_params=pltpu.CompilerParams(
            collective_id=1, has_side_effects=True, vmem_limit_bytes=50 * 2**20
        ),
        name="block",
    )(pick, tokens, w, wt, out_w)


def per_device(tokens, key_frame, qkv_spatial, out_spatial, qkv_temporal):
    frame = lax.axis_index("frame")
    key = key_frame[0].astype(jnp.int32)
    y, zl, core = frame // 8, (frame // 2) % 4, frame % 2
    pick = jnp.stack(
        [(key // 8 - y) % 4 * 2 + (key % 2 - core) % 2, (key // 2 % 4 - zl) % 4]
    ).astype(jnp.int32)
    spatial, temporal = block(
        pick, tokens[0], qkv_spatial, qkv_temporal, out_spatial
    )
    return (spatial[None], temporal[None])


def solution(mesh):
    return jax.shard_map(
        per_device,
        mesh=mesh,
        in_specs=(P("frame", "patch", None), P(), P(None, "patch"), P(), P(None, "patch")),
        out_specs=(P("frame", "patch", None), P("frame", "patch", None)),
        check_vma=False,
    )
```
